256 devices in a mesh: chan: 16 (over z, core), cross: 16 (over x, y).
Axes of the slice: x: 4, y: 4, z: 8, core: 2. Of those that a mesh axis runs over, the one named last changes fastest.
Arguments:
- tracers: float32 [5, 4, 256, 32768], P(None, None, 'chan', 'cross'), may hold values from 0 to 10
- kappa_x: float32 [4, 256, 32768], P(None, 'chan', 'cross'), may hold values from 0.5 to 50
- kappa_y: float32 [4, 256, 32768], P(None, 'chan', 'cross'), may hold values from 0.05 to 0.24
- courant: float32 [4, 256, 32768], P(None, 'chan', 'cross'), may hold values from 32 to 320
- wet_mask: int32 [256, 32768], P('chan', 'cross'), may hold values from 0 to 1, as said below
- levels: int32 [256, 32768], P('chan', 'cross'), may hold values from 2 to 4, as said below
Outputs:
- updated: float32 [5, 4, 256, 32768], P(None, None, 'chan', 'cross')
The draws below stay inside these ranges and needn't reach their ends.
Inputs may be any that keep to these rules, and one draw needn't show every extreme that they name: `wet_mask`: for every along-channel cell the dry cells are the first 1 to 2048 and the last 1 to 2048 cross-channel cells; all others are wet. `levels`: the layer count of a column depends only on its cross-channel cell.
All inputs are finite; a program needn't handle non-finite values.
Results may differ from the reference program's by a relative error of at most 0.000042.
Values sent between devices are 32-bit elements; how exact they have to be, the bound alone decides.
No kernel may reach another device: no remote copies, remote signals or barrier semaphores. Data moves between devices by JAX's collectives and lax.ppermute only.
A program may use at most 128 MiB of HBM per device.

```python
import math
import jax
import jax.numpy as jnp
from jax import lax

TRACERS = 5
LAYERS = 4
NX = 256
NY = 32768


def draw_tracers(key, part):
    key = jax.random.fold_in(key, 11)
    keys = jax.random.split(key, 5)
    small = (TRACERS, 1, 1, 1)
    level = jax.random.uniform(keys[0], small, jnp.float32, 0.9, 1.5)
    swing = jax.random.uniform(keys[1], small, jnp.float32, 0.3, 0.7)
    waves = jax.random.uniform(keys[2], small, jnp.float32, 0.5, 1.5)
    noise = jax.random.normal(keys[4], (TRACERS, LAYERS, NX, NY), jnp.float32)
    rough = jnp.exp(0.5 * jnp.clip(noise, -3.0, 3.0))
    phase = jax.random.uniform(keys[3], (TRACERS, LAYERS, 1, 1), jnp.float32, -math.pi, math.pi)
    along = (jnp.arange(NX, dtype=jnp.float32) / NX)[None, None, :, None]
    smooth = level + swing * jnp.sin(2.0 * math.pi * waves * along + phase)
    return (smooth * rough).astype(jnp.float32)


def draw_wet_mask(key, part):
    key = jax.random.fold_in(key, 23)
    key_low, key_high = jax.random.split(key, 2)
    widest = NY // 16
    along = jnp.arange(NX, dtype=jnp.int32)[:, None]
    bank_low = jax.random.randint(key_low, (NX, 1), 1, widest + 1, dtype=jnp.int32)
    bank_high = jax.random.randint(key_high, (NX, 1), 1, widest + 1, dtype=jnp.int32)
    bank_low = jnp.where(along == 0, widest, bank_low)
    bank_high = jnp.where(along == NX - 1, widest, bank_high)
    across = jnp.arange(NY, dtype=jnp.int32)[None, :]
    wet = (across >= bank_low) & (across < NY - bank_high)
    return wet.astype(jnp.int32)


def draw_levels(key, part):
    key = jax.random.fold_in(key, 37)
    depth = jax.random.randint(key, (NY,), 2, LAYERS + 1, dtype=jnp.int32)
    across = jnp.arange(NY, dtype=jnp.int32)
    depth = jnp.where(across == NY // 2, LAYERS, jnp.where(across == 0, 2, depth))
    return jnp.broadcast_to(depth[None, :], (NX, NY)).astype(jnp.int32)


def shard_levels(stream_key, extent, cuts, least, largest):
    def one(axis_at, parts):
        draws = jax.random.uniform(jax.random.fold_in(jax.random.fold_in(stream_key, 6), axis_at), (parts,), jnp.float32, least / len(cuts), largest / len(cuts))
        return jnp.repeat(jnp.exp(draws), extent[axis_at] // parts).reshape((-1,) + (1,) * (len(extent) - axis_at - 1))

    loudness = one(*cuts[0])
    for cut in cuts[1:]:
        loudness = loudness * one(*cut)
    return loudness


def setup_inputs(seed: int = 0) -> dict:
    key_list = jax.random.split(jax.random.key(seed), 7)
    return {
        "tracers": draw_tracers(jax.random.fold_in(key_list[6], 71), 0),
        "kappa_x": jnp.clip(jnp.exp(math.log(50.0) - 4.6051702 * jax.random.uniform(key_list[1], (LAYERS, NX, NY), jnp.float32) ** shard_levels(key_list[1], (LAYERS, NX, NY), ((1, 16), (2, 16)), -0.2, 0.2)), 0.5, 50.0),
        "kappa_y": jnp.clip(jnp.exp(math.log(0.24) - 1.5686159 * jax.random.uniform(key_list[2], (LAYERS, NX, NY), jnp.float32) ** shard_levels(key_list[2], (LAYERS, NX, NY), ((1, 16), (2, 16)), -0.2, 0.2)), 0.05, 0.24),
        "courant": jnp.clip(jnp.exp(math.log(320.0) - 2.3025851 * jax.random.uniform(key_list[3], (LAYERS, NX, NY), jnp.float32) ** shard_levels(key_list[3], (LAYERS, NX, NY), ((1, 16), (2, 16)), -0.2, 0.2)), 32.0, 320.0),
        "wet_mask": draw_wet_mask(jax.random.fold_in(key_list[6], 71), 0),
        "levels": draw_levels(jax.random.fold_in(key_list[6], 71), 0),
    }


def assemble(tracers, kappa_x, kappa_y, courant, wet_mask, levels):
    layer_ids = lax.broadcasted_iota(jnp.int32, kappa_x.shape, 0)
    active = ((wet_mask[None] > 0) & (layer_ids < levels[None])).astype(jnp.float32)
    cross_diff = kappa_y * active
    chan_diff = kappa_x * active
    padded_tr = jnp.pad(tracers, ((0, 0), (0, 0), (0, 0), (1, 1)))
    padded_cd = jnp.pad(cross_diff, ((0, 0), (0, 0), (1, 1)))
    upper_face = jnp.minimum(padded_cd[:, :, 1:-1], padded_cd[:, :, 2:])
    lower_face = jnp.minimum(padded_cd[:, :, 1:-1], padded_cd[:, :, :-2])
    centre = padded_tr[..., 1:-1]
    right_side = centre + upper_face * (padded_tr[..., 2:] - centre) - lower_face * (centre - padded_tr[..., :-2])
    padded_xd = jnp.pad(chan_diff, ((0, 0), (1, 1), (0, 0)))
    padded_act = jnp.pad(active, ((0, 0), (1, 1), (0, 0)))
    face_up = jnp.minimum(padded_xd[:, 1:-1], padded_xd[:, 2:])
    face_down = jnp.minimum(padded_xd[:, 1:-1], padded_xd[:, :-2])
    inflow = courant * padded_act[:, :-2]
    lower_band = -active * (face_down + inflow)
    upper_band = -active * face_up
    main_band = 1.0 + active * (face_down + face_up + inflow)
    return lower_band, main_band, upper_band, right_side


def reference(tracers, kappa_x, kappa_y, courant, wet_mask, levels):
    lower_band, main_band, upper_band, right_side = assemble(tracers, kappa_x, kappa_y, courant, wet_mask, levels)
    lower_rows = jnp.moveaxis(lower_band, 1, 0)
    main_rows = jnp.moveaxis(main_band, 1, 0)
    upper_rows = jnp.moveaxis(upper_band, 1, 0)
    side_rows = jnp.moveaxis(right_side, 2, 0)

    def forward(carry, row):
        ratio_prev, reduced_prev = carry
        lower_row, main_row, upper_row, side_row = row
        pivot = main_row - lower_row * ratio_prev
        ratio = upper_row / pivot
        reduced = (side_row - lower_row[None] * reduced_prev) / pivot[None]
        return (ratio, reduced), (ratio, reduced)

    start = (jnp.zeros(main_rows.shape[1:], jnp.float32), jnp.zeros(side_rows.shape[1:], jnp.float32))
    unused, (ratios, reduceds) = lax.scan(forward, start, (lower_rows, main_rows, upper_rows, side_rows))

    def backward(following, row):
        ratio, reduced = row
        value = reduced - ratio[None] * following
        return value, value

    unused_last, values = lax.scan(backward, jnp.zeros(side_rows.shape[1:], jnp.float32), (ratios, reduceds), reverse=True)
    return jnp.moveaxis(values, 0, 2)
```

```python
import functools

import jax
import jax.numpy as jnp
from jax import lax
from jax.experimental import pallas as pl
from jax.experimental.pallas import tpu as pltpu
from jax.sharding import PartitionSpec as P

TRACERS = 5
LAYERS = 4
ROWS = 16
CHIPS = 8
CD0, WA0, D0, F0, R0, CDN, DN, EN, RN = 0, 1, 2, 3, 4, 9, 10, 11, 12
PARTS = 17
SENT = 18
BACK = 10
F32 = jnp.float32


def folded(cells):
    lead = cells.shape[:-2]
    cells = cells.reshape(lead + (2, 8, 16, 128))
    return jnp.swapaxes(cells, len(lead) + 1, len(lead) + 2).reshape(lead + (256, 128))


def unfolded(cells):
    lead = cells.shape[:-2]
    cells = cells.reshape(lead + (2, 16, 8, 128))
    return jnp.swapaxes(cells, len(lead) + 1, len(lead) + 2).reshape(lead + (16, 2048))


def line(row, half):
    return pl.ds((row // 8) * 128 + half * 64 + row % 8, 8, stride=8)


def tile(row_tile, column_tile):
    return pl.ds(row_tile * 128 + column_tile * 8, 8)


def edges_kernel(tr_lo, tr_hi, ky_lo, ky_hi, wet_lo, wet_hi, lev_lo, lev_hi, out_lo, out_hi):
    lane = lax.broadcasted_iota(jnp.int32, (8, 128), 1)
    for tr, ky, wet, lev, out, at in (
        (tr_lo, ky_lo, wet_lo, lev_lo, out_lo, 0),
        (tr_hi, ky_hi, wet_hi, lev_hi, out_hi, 127),
    ):
        for l in range(LAYERS):
            for i in range(2):
                rows = pl.ds(i * 8, 8)
                active = (wet[rows, :] > 0) & (lev[rows, :] > l)
                parts = [tr[t, l, rows, :] for t in range(TRACERS)]
                parts.append(jnp.where(active, ky[l, rows, :], 0.0))
                packed = jnp.zeros((8, 128), F32)
                for t, part in enumerate(parts):
                    packed = jnp.where(lane == t, pltpu.roll(part, (t - at) % 128, 1), packed)
                out[l, rows, :] = packed


def edges(tracers, kappa_y, wet, levels):
    def spec(lead, at):
        zeros = (0,) * (len(lead) + 1)
        return pl.BlockSpec(lead + (16, 128), lambda i, zeros=zeros, at=at: zeros + (at,))

    return pl.pallas_call(
        edges_kernel,
        grid=(1,),
        in_specs=[
            spec((TRACERS, LAYERS), 0),
            spec((TRACERS, LAYERS), 15),
            spec((LAYERS,), 0),
            spec((LAYERS,), 15),
            spec((), 0),
            spec((), 15),
            spec((), 0),
            spec((), 15),
        ],
        out_specs=[pl.BlockSpec((LAYERS, 16, 128), lambda i: (0, 0, 0))] * 2,
        out_shape=[jax.ShapeDtypeStruct((LAYERS, 16, 128), F32)] * 2,
        name="edges",
    )(tracers, tracers, kappa_y, kappa_y, wet, wet, levels, levels)


def local_kernel(
    core, tr, kx, ky, co, wet, lev, left, right, red, fill, rho, mine, theirs, side
):
    layer = pl.program_id(0)
    first_core = core[0] == 0
    lane = lax.broadcasted_iota(jnp.int32, (8, 128), 1)
    head, tail = lane == 0, lane == 127

    for i in range(2):
        rows = pl.ds(i * 8, 8)
        lo, hi = left[0, rows, :], right[0, rows, :]

        def cross_of(j):
            active = (wet[tile(i, j), :] > 0) & (lev[tile(i, j), :] > layer)
            return jnp.where(active, ky[0, tile(i, j), :], 0.0)

        def ahead(now, following):
            return jnp.where(tail, pltpu.roll(following, 127, 1), pltpu.roll(now, 127, 1))

        faces = []
        now = cross_of(0)
        first_face = jnp.minimum(now, pltpu.roll(lo, (0 - TRACERS) % 128, 1))
        for j in range(16):
            following = cross_of(j + 1) if j < 15 else pltpu.roll(hi, (0 - TRACERS) % 128, 1)
            faces.append(jnp.minimum(now, ahead(now, following)))
            now = following
        for t in range(TRACERS):
            now = tr[t, 0, tile(i, 0), :]
            shifted = pltpu.roll(now, 127, 1)
            before = first_face * (now - pltpu.roll(lo, (0 - t) % 128, 1))
            for j in range(16):
                following = tr[t, 0, tile(i, j + 1), :] if j < 15 else pltpu.roll(hi, (0 - t) % 128, 1)
                shifted_following = pltpu.roll(following, 127, 1)
                flux = faces[j] * (jnp.where(tail, shifted_following, shifted) - now)
                behind = pltpu.roll(flux, 1, 1)
                side[t, tile(i, j), :] = now + flux - jnp.where(head, before, behind)
                before = behind
                now, shifted = following, shifted_following

    halves = []
    for half in range(2):

        def load(row):
            where = line(row, half)
            active = (wet[where, :] > 0) & (lev[where, :] > layer)
            act = jnp.where(active, 1.0, 0.0).astype(F32)
            return act, kx[0, where, :] * act, co[0, where, :]

        out = [None] * PARTS
        act_prev, cd_prev, co_prev = load(0)
        act, cd, cour = load(1)
        out[CD0] = cd_prev
        out[WA0] = act_prev * co_prev
        face_first = jnp.minimum(cd_prev, cd)
        face_down = face_first
        rho_row = None
        for row in range(1, ROWS - 1):
            act_next, cd_next, co_next = load(row + 1)
            face_up = jnp.minimum(cd, cd_next)
            low = act * (face_down + cour * act_prev)
            where = pl.ds((half * ROWS + row) * 8, 8)
            if row == 1:
                inverse = 1.0 / (1.0 + face_up + low)
                rho_row = face_up * inverse
                gain = low * inverse
                fill_row = gain
                reds = [side[t, line(row, half), :] * inverse for t in range(TRACERS)]
                sums = list(reds)
                sum_fill = fill_row
                chain = rho_row
            else:
                inverse = 1.0 / (1.0 + face_up + low * (1.0 - rho_row))
                rho_row = face_up * inverse
                gain = low * inverse
                fill_row = gain * fill_row
                reds = [side[t, line(row, half), :] * inverse + gain * reds[t] for t in range(TRACERS)]
                sums = [sums[t] + chain * reds[t] for t in range(TRACERS)]
                sum_fill = sum_fill + chain * fill_row
                chain = chain * rho_row
            rho[0, where, :] = rho_row
            fill[0, where, :] = fill_row
            for t in range(TRACERS):
                red[t, 0, where, :] = reds[t]
            act_prev = act
            act, cd, cour = act_next, cd_next, co_next
            face_down = face_up
        low = act * (face_down + cour * act_prev)
        out[D0] = 1.0 + face_first * (1.0 - sum_fill)
        out[F0] = face_first * chain
        out[CDN] = cd
        out[DN] = 1.0 + low * (1.0 - rho_row)
        out[EN] = low * fill_row
        for t in range(TRACERS):
            out[R0 + t] = side[t, line(0, half), :] + face_first * sums[t]
            out[RN + t] = side[t, line(ROWS - 1, half), :] + low * reds[t]
        halves.append(out)
    for part in range(PARTS):
        mine[part, 0] = jnp.where(first_core, halves[0][part], halves[1][part])
        theirs[part, 0] = jnp.where(first_core, halves[1][part], halves[0][part])


def local_part(core, tracers, kappa_x, kappa_y, courant, wet, levels, left, right):
    layered = lambda *lead: pl.BlockSpec(lead + (1, 256, 128), lambda l, n=len(lead): (0,) * n + (l, 0, 0))
    whole = pl.BlockSpec((256, 128), lambda l: (0, 0))
    halo = pl.BlockSpec((1, 16, 128), lambda l: (l, 0, 0))
    packed = pl.BlockSpec((PARTS, 1, 8, 128), lambda l: (0, l, 0, 0))
    return pl.pallas_call(
        local_kernel,
        grid=(LAYERS,),
        in_specs=[
            pl.BlockSpec(memory_space=pltpu.SMEM),
            layered(TRACERS),
            layered(),
            layered(),
            layered(),
            whole,
            whole,
            halo,
            halo,
        ],
        out_specs=[layered(TRACERS), layered(), layered(), packed, packed],
        out_shape=[
            jax.ShapeDtypeStruct((TRACERS, LAYERS, 256, 128), F32),
            jax.ShapeDtypeStruct((LAYERS, 256, 128), F32),
            jax.ShapeDtypeStruct((LAYERS, 256, 128), F32),
            jax.ShapeDtypeStruct((PARTS, LAYERS, 8, 128), F32),
            jax.ShapeDtypeStruct((PARTS, LAYERS, 8, 128), F32),
        ],
        scratch_shapes=[pltpu.VMEM((TRACERS, 256, 128), F32)],
        compiler_params=pltpu.CompilerParams(vmem_limit_bytes=16 * 1024 * 1024),
        name="local_part",
    )(core, tracers, kappa_x, kappa_y, courant, wet, levels, left, right)


def pair_kernel(core, mine, other, sent, kept):
    first_core = core[0] == 0
    for l in range(LAYERS):
        a = [mine[part, l] for part in range(PARTS)]
        b = [other[part, l] for part in range(PARTS)]
        lo = [jnp.where(first_core, x, y) for x, y in zip(a, b)]
        hi = [jnp.where(first_core, y, x) for x, y in zip(a, b)]
        face = jnp.minimum(lo[CDN], hi[CD0])
        down = face + jnp.where(lo[CDN] > 0.0, hi[WA0], 0.0)
        scale = 1.0 / (lo[DN] * (hi[D0] + down) + face * hi[D0])
        in_b = scale * (hi[D0] + down)
        in_g = scale * face
        in_w = scale * down
        in_a = scale * (lo[DN] + face)
        last_f, last_l = in_b * lo[EN], in_g * hi[F0]
        first_f, first_l = in_w * lo[EN], in_a * hi[F0]
        last_r = [in_b * lo[RN + t] + in_g * hi[R0 + t] for t in range(TRACERS)]
        first_r = [in_w * lo[RN + t] + in_a * hi[R0 + t] for t in range(TRACERS)]
        out = [None] * PARTS
        out[CD0], out[WA0], out[CDN] = lo[CD0], lo[WA0], hi[CDN]
        out[D0] = lo[D0] - lo[F0] * last_f
        out[F0] = lo[F0] * last_l
        out[DN] = hi[DN] - hi[EN] * first_l
        out[EN] = hi[EN] * first_f
        for t in range(TRACERS):
            out[R0 + t] = lo[R0 + t] + lo[F0] * last_r[t]
            out[RN + t] = hi[RN + t] + hi[EN] * first_r[t]
        for part in range(PARTS):
            sent[pl.ds(l * SENT + part, CHIPS, stride=LAYERS * SENT), :] = out[part]
        sent[pl.ds(l * SENT + PARTS, CHIPS, stride=LAYERS * SENT), :] = jnp.zeros((8, 128), F32)
        for k, value in enumerate(last_r + first_r + [last_f, last_l, first_f, first_l]):
            kept[k, l] = value


def pair_part(core, mine, other):
    vmem = pl.BlockSpec(memory_space=pltpu.VMEM)
    return pl.pallas_call(
        pair_kernel,
        in_specs=[pl.BlockSpec(memory_space=pltpu.SMEM), vmem, vmem],
        out_specs=[vmem, vmem],
        out_shape=[
            jax.ShapeDtypeStruct((CHIPS * LAYERS * SENT, 128), F32),
            jax.ShapeDtypeStruct((14, LAYERS, 8, 128), F32),
        ],
        name="pair_part",
    )(core, mine, other)


def chain_kernel(parts, solved):
    load = lambda chip, part: parts[pl.ds(chip * LAYERS * SENT + part, LAYERS, stride=SENT), :]
    firsts, lasts = [], []
    cd_prev = gate = ratio = reduced = None
    base, known = None, None
    for chip in range(CHIPS):
        d0, f0 = load(chip, D0), load(chip, F0)
        dn, en = load(chip, DN), load(chip, EN)
        r0 = [load(chip, R0 + t) for t in range(TRACERS)]
        rn = [load(chip, RN + t) for t in range(TRACERS)]
        if chip:
            cd0 = load(chip, CD0)
            face = jnp.minimum(cd_prev, cd0)
            down = face + jnp.where(cd_prev > 0.0, load(chip, WA0), 0.0)
            inverse = 1.0 / (base + face)
            ratio = face * inverse
            reduced = [x * inverse for x in known]
            lasts.append((ratio, reduced))
            inverse = 1.0 / (d0 + down * (1.0 - ratio))
            r0 = [x + down * y for x, y in zip(r0, reduced)]
        else:
            inverse = 1.0 / d0
        ahead = f0 * inverse
        here = [x * inverse for x in r0]
        firsts.append((ahead, here))
        base = dn - en * ahead
        known = [x + en * y for x, y in zip(rn, here)]
        cd_prev = load(chip, CDN)
    inverse = 1.0 / base
    last = [x * inverse for x in known]
    for chip in reversed(range(CHIPS)):
        ahead, here = firsts[chip]
        first = [x + ahead * y for x, y in zip(here, last)]
        for t in range(TRACERS):
            solved[pl.ds(chip * LAYERS * BACK + t, LAYERS, stride=BACK), :] = first[t]
            solved[pl.ds(chip * LAYERS * BACK + TRACERS + t, LAYERS, stride=BACK), :] = last[t]
        if chip:
            ratio, reduced = lasts[chip - 1]
            last = [x + ratio * y for x, y in zip(reduced, first)]


def chain_part(parts):
    vmem = pl.BlockSpec(memory_space=pltpu.VMEM)
    return pl.pallas_call(
        chain_kernel,
        in_specs=[vmem],
        out_specs=vmem,
        out_shape=jax.ShapeDtypeStruct((CHIPS * LAYERS * BACK, 128), F32),
        name="chain_part",
    )(parts)


def middle_kernel(core, solved, kept, mine, theirs):
    first_core = core[0] == 0
    for l in range(LAYERS):
        last_f, last_l, first_f, first_l = (kept[10 + k, l] for k in range(4))
        for t in range(TRACERS):
            first = solved[pl.ds(l * BACK + t, CHIPS, stride=LAYERS * BACK), :]
            last = solved[pl.ds(l * BACK + TRACERS + t, CHIPS, stride=LAYERS * BACK), :]
            before = kept[t, l] + last_f * first + last_l * last
            after = kept[TRACERS + t, l] + first_f * first + first_l * last
            mine[t, l] = jnp.where(first_core, first, after)
            mine[TRACERS + t, l] = jnp.where(first_core, before, last)
            theirs[t, l] = jnp.where(first_core, after, first)
            theirs[TRACERS + t, l] = jnp.where(first_core, last, before)


def middle_part(core, solved, kept):
    vmem = pl.BlockSpec(memory_space=pltpu.VMEM)
    return pl.pallas_call(
        middle_kernel,
        in_specs=[pl.BlockSpec(memory_space=pltpu.SMEM), vmem, vmem],
        out_specs=[vmem, vmem],
        out_shape=[jax.ShapeDtypeStruct((BACK, LAYERS, 8, 128), F32)] * 2,
        name="middle_part",
    )(core, solved, kept)


def final_kernel(core, red, fill, rho, mine, other, out):
    first_core = core[0] == 0
    for half in range(2):
        pick = (lambda k: jnp.where(first_core, mine[k, 0], other[k, 0])) if half == 0 else (
            lambda k: jnp.where(first_core, other[k, 0], mine[k, 0])
        )
        firsts = [pick(t) for t in range(TRACERS)]
        cells = [pick(TRACERS + t) for t in range(TRACERS)]
        for t in range(TRACERS):
            out[t, 0, line(ROWS - 1, half), :] = cells[t]
            out[t, 0, line(0, half), :] = firsts[t]
        for row in reversed(range(1, ROWS - 1)):
            where = pl.ds((half * ROWS + row) * 8, 8)
            fill_row, rho_row = fill[0, where, :], rho[0, where, :]
            for t in range(TRACERS):
                cells[t] = red[t, 0, where, :] + fill_row * firsts[t] + rho_row * cells[t]
                out[t, 0, line(row, half), :] = cells[t]


def final_part(core, red, fill, rho, mine, other):
    layered = lambda *lead: pl.BlockSpec(lead + (1, 256, 128), lambda l, n=len(lead): (0,) * n + (l, 0, 0))
    packed = pl.BlockSpec((BACK, 1, 8, 128), lambda l: (0, l, 0, 0))
    return pl.pallas_call(
        final_kernel,
        grid=(LAYERS,),
        in_specs=[
            pl.BlockSpec(memory_space=pltpu.SMEM),
            layered(TRACERS),
            layered(),
            layered(),
            packed,
            packed,
        ],
        out_specs=layered(TRACERS),
        out_shape=jax.ShapeDtypeStruct((TRACERS, LAYERS, 256, 128), F32),
        compiler_params=pltpu.CompilerParams(vmem_limit_bytes=16 * 1024 * 1024),
        name="final_part",
    )(core, red, fill, rho, mine, other)


def on_device(tracers, kappa_x, kappa_y, courant, wet_mask, levels):
    count = lax.axis_size("cross")
    core = (lax.axis_index("chan") % 2).astype(jnp.int32).reshape(1)
    pairs = [(i, i ^ 1) for i in range(2 * CHIPS)]
    lines = [[c + 2 * z for z in range(CHIPS)] for c in range(2)]

    lowest, highest = edges(tracers, kappa_y, wet_mask, levels)
    left = lax.ppermute(highest, "cross", [(i, i + 1) for i in range(count - 1)])
    right = lax.ppermute(lowest, "cross", [(i + 1, i) for i in range(count - 1)])
    red, fill, rho, mine, theirs = local_part(
        core,
        folded(tracers),
        folded(kappa_x),
        folded(kappa_y),
        folded(courant),
        folded(wet_mask),
        folded(levels),
        left,
        right,
    )
    other = lax.ppermute(theirs, "chan", pairs)
    sent, kept = pair_part(core, mine, other)
    parts = lax.all_to_all(
        sent.reshape(CHIPS, LAYERS * SENT, 128), "chan", 0, 0, axis_index_groups=lines, tiled=True
    )
    solved = chain_part(parts.reshape(CHIPS * LAYERS * SENT, 128))
    back = lax.all_to_all(
        solved.reshape(CHIPS, LAYERS * BACK, 128), "chan", 0, 0, axis_index_groups=lines, tiled=True
    )
    mine, theirs = middle_part(core, back.reshape(CHIPS * LAYERS * BACK, 128), kept)
    other = lax.ppermute(theirs, "chan", pairs)
    return unfolded(final_part(core, red, fill, rho, mine, other))


def solution(mesh):
    placed = (
        P(None, None, "chan", "cross"),
        P(None, "chan", "cross"),
        P(None, "chan", "cross"),
        P(None, "chan", "cross"),
        P("chan", "cross"),
        P("chan", "cross"),
    )
    return jax.shard_map(
        on_device,
        mesh=mesh,
        in_specs=placed,
        out_specs=P(None, None, "chan", "cross"),
        check_vma=False,
    )
```

```python
import functools

import jax
import jax.numpy as jnp
from jax import lax
from jax.experimental import pallas as pl
from jax.experimental.pallas import tpu as pltpu
from jax.sharding import PartitionSpec as P

TRACERS = 5
LAYERS = 4
ROWS = 16
CHIPS = 8
CD0, WA0, D0, F0, R0, CDN, DN, EN, RN = 0, 1, 2, 3, 4, 9, 10, 11, 12
PARTS = 17
SENT = 18
BACK = 10
F32 = jnp.float32
SMALL = pltpu.CompilerParams(vmem_limit_bytes=4 * 1024 * 1024)


def folded(cells):
    lead = cells.shape[:-2]
    cells = cells.reshape(lead + (2, 8, 16, 128))
    return jnp.swapaxes(cells, len(lead) + 1, len(lead) + 2).reshape(lead + (256, 128))


def unfolded(cells):
    lead = cells.shape[:-2]
    cells = cells.reshape(lead + (2, 16, 8, 128))
    return jnp.swapaxes(cells, len(lead) + 1, len(lead) + 2).reshape(lead + (16, 2048))


def line(row, half):
    return pl.ds((row // 8) * 128 + half * 64 + row % 8, 8, stride=8)


def tile(row_tile, column_tile):
    return pl.ds(row_tile * 128 + column_tile * 8, 8)


def edges_kernel(tr_lo, tr_hi, ky_lo, ky_hi, wet_lo, wet_hi, lev_lo, lev_hi, out_lo, out_hi):
    lane = lax.broadcasted_iota(jnp.int32, (8, 128), 1)
    for tr, ky, wet, lev, out, at in (
        (tr_lo, ky_lo, wet_lo, lev_lo, out_lo, 0),
        (tr_hi, ky_hi, wet_hi, lev_hi, out_hi, 127),
    ):
        for l in range(LAYERS):
            for i in range(2):
                rows = pl.ds(i * 8, 8)
                active = (wet[rows, :] > 0) & (lev[rows, :] > l)
                parts = [tr[t, l, rows, :] for t in range(TRACERS)]
                parts.append(jnp.where(active, ky[l, rows, :], 0.0))
                packed = jnp.zeros((8, 128), F32)
                for t, part in enumerate(parts):
                    packed = jnp.where(lane == t, pltpu.roll(part, (t - at) % 128, 1), packed)
                out[l, rows, :] = packed


def edges(tracers, kappa_y, wet, levels):
    def spec(lead, at):
        zeros = (0,) * (len(lead) + 1)
        return pl.BlockSpec(lead + (16, 128), lambda i, zeros=zeros, at=at: zeros + (at,))

    return pl.pallas_call(
        edges_kernel,
        grid=(1,),
        in_specs=[
            spec((TRACERS, LAYERS), 0),
            spec((TRACERS, LAYERS), 15),
            spec((LAYERS,), 0),
            spec((LAYERS,), 15),
            spec((), 0),
            spec((), 15),
            spec((), 0),
            spec((), 15),
        ],
        out_specs=[pl.BlockSpec((LAYERS, 16, 128), lambda i: (0, 0, 0))] * 2,
        out_shape=[jax.ShapeDtypeStruct((LAYERS, 16, 128), F32)] * 2,
        compiler_params=SMALL,
        name="edges",
    )(tracers, tracers, kappa_y, kappa_y, wet, wet, levels, levels)


def local_kernel(
    core, tr, kx, ky, co, wet, lev, left, right, red, fill, rho, mine, theirs, side
):
    lax.fori_loop(
        0,
        LAYERS,
        lambda layer, none: local_layer(
            layer, core, tr, kx, ky, co, wet, lev, left, right, red, fill, rho, mine, theirs, side
        ),
        None,
    )


def local_layer(
    layer, core, tr, kx, ky, co, wet, lev, left, right, red, fill, rho, mine, theirs, side
):
    first_core = core[0] == 0
    lane = lax.broadcasted_iota(jnp.int32, (8, 128), 1)
    head, tail = lane == 0, lane == 127

    for i in range(2):
        rows = pl.ds(i * 8, 8)
        lo, hi = left[layer, rows, :], right[layer, rows, :]

        def cross_of(j):
            active = (wet[tile(i, j), :] > 0) & (lev[tile(i, j), :] > layer)
            return jnp.where(active, ky[layer, tile(i, j), :], 0.0)

        def ahead(now, following):
            return jnp.where(tail, pltpu.roll(following, 127, 1), pltpu.roll(now, 127, 1))

        faces = []
        now = cross_of(0)
        first_face = jnp.minimum(now, pltpu.roll(lo, (0 - TRACERS) % 128, 1))
        for j in range(16):
            following = cross_of(j + 1) if j < 15 else pltpu.roll(hi, (0 - TRACERS) % 128, 1)
            faces.append(jnp.minimum(now, ahead(now, following)))
            now = following
        for t in range(TRACERS):
            now = tr[t, layer, tile(i, 0), :]
            shifted = pltpu.roll(now, 127, 1)
            before = first_face * (now - pltpu.roll(lo, (0 - t) % 128, 1))
            for j in range(16):
                following = tr[t, layer, tile(i, j + 1), :] if j < 15 else pltpu.roll(hi, (0 - t) % 128, 1)
                shifted_following = pltpu.roll(following, 127, 1)
                flux = faces[j] * (jnp.where(tail, shifted_following, shifted) - now)
                behind = pltpu.roll(flux, 1, 1)
                side[t, tile(i, j), :] = now + flux - jnp.where(head, before, behind)
                before = behind
                now, shifted = following, shifted_following

    halves = []
    for half in range(2):

        def load(row):
            where = line(row, half)
            active = (wet[where, :] > 0) & (lev[where, :] > layer)
            act = jnp.where(active, 1.0, 0.0).astype(F32)
            return act, kx[layer, where, :] * act, co[layer, where, :]

        out = [None] * PARTS
        act_prev, cd_prev, co_prev = load(0)
        act, cd, cour = load(1)
        out[CD0] = cd_prev
        out[WA0] = act_prev * co_prev
        face_first = jnp.minimum(cd_prev, cd)
        face_down = face_first
        rho_row = None
        for row in range(1, ROWS - 1):
            act_next, cd_next, co_next = load(row + 1)
            face_up = jnp.minimum(cd, cd_next)
            low = act * (face_down + cour * act_prev)
            where = pl.ds((half * ROWS + row) * 8, 8)
            if row == 1:
                inverse = 1.0 / (1.0 + face_up + low)
                rho_row = face_up * inverse
                gain = low * inverse
                fill_row = gain
                reds = [side[t, line(row, half), :] * inverse for t in range(TRACERS)]
                sums = list(reds)
                sum_fill = fill_row
                chain = rho_row
            else:
                inverse = 1.0 / (1.0 + face_up + low * (1.0 - rho_row))
                rho_row = face_up * inverse
                gain = low * inverse
                fill_row = gain * fill_row
                reds = [side[t, line(row, half), :] * inverse + gain * reds[t] for t in range(TRACERS)]
                sums = [sums[t] + chain * reds[t] for t in range(TRACERS)]
                sum_fill = sum_fill + chain * fill_row
                chain = chain * rho_row
            rho[layer, where, :] = rho_row
            fill[layer, where, :] = fill_row
            for t in range(TRACERS):
                red[t, layer, where, :] = reds[t]
            act_prev = act
            act, cd, cour = act_next, cd_next, co_next
            face_down = face_up
        low = act * (face_down + cour * act_prev)
        out[D0] = 1.0 + face_first * (1.0 - sum_fill)
        out[F0] = face_first * chain
        out[CDN] = cd
        out[DN] = 1.0 + low * (1.0 - rho_row)
        out[EN] = low * fill_row
        for t in range(TRACERS):
            out[R0 + t] = side[t, line(0, half), :] + face_first * sums[t]
            out[RN + t] = side[t, line(ROWS - 1, half), :] + low * reds[t]
        halves.append(out)
    for part in range(PARTS):
        mine[part, layer] = jnp.where(first_core, halves[0][part], halves[1][part])
        theirs[part, layer] = jnp.where(first_core, halves[1][part], halves[0][part])


def local_part(core, tracers, kappa_x, kappa_y, courant, wet, levels, left, right):
    vmem = pl.BlockSpec(memory_space=pltpu.VMEM)
    return pl.pallas_call(
        local_kernel,
        in_specs=[pl.BlockSpec(memory_space=pltpu.SMEM)] + [vmem] * 8,
        out_specs=[vmem] * 5,
        out_shape=[
            jax.ShapeDtypeStruct((TRACERS, LAYERS, 256, 128), F32),
            jax.ShapeDtypeStruct((LAYERS, 256, 128), F32),
            jax.ShapeDtypeStruct((LAYERS, 256, 128), F32),
            jax.ShapeDtypeStruct((PARTS, LAYERS, 8, 128), F32),
            jax.ShapeDtypeStruct((PARTS, LAYERS, 8, 128), F32),
        ],
        scratch_shapes=[pltpu.VMEM((TRACERS, 256, 128), F32)],
        compiler_params=pltpu.CompilerParams(vmem_limit_bytes=12 * 1024 * 1024),
        name="local_part",
    )(core, tracers, kappa_x, kappa_y, courant, wet, levels, left, right)


def pair_kernel(core, mine, other, sent, kept):
    first_core = core[0] == 0
    for l in range(LAYERS):
        a = [mine[part, l] for part in range(PARTS)]
        b = [other[part, l] for part in range(PARTS)]
        lo = [jnp.where(first_core, x, y) for x, y in zip(a, b)]
        hi = [jnp.where(first_core, y, x) for x, y in zip(a, b)]
        face = jnp.minimum(lo[CDN], hi[CD0])
        down = face + jnp.where(lo[CDN] > 0.0, hi[WA0], 0.0)
        scale = 1.0 / (lo[DN] * (hi[D0] + down) + face * hi[D0])
        in_b = scale * (hi[D0] + down)
        in_g = scale * face
        in_w = scale * down
        in_a = scale * (lo[DN] + face)
        last_f, last_l = in_b * lo[EN], in_g * hi[F0]
        first_f, first_l = in_w * lo[EN], in_a * hi[F0]
        last_r = [in_b * lo[RN + t] + in_g * hi[R0 + t] for t in range(TRACERS)]
        first_r = [in_w * lo[RN + t] + in_a * hi[R0 + t] for t in range(TRACERS)]
        out = [None] * PARTS
        out[CD0], out[WA0], out[CDN] = lo[CD0], lo[WA0], hi[CDN]
        out[D0] = lo[D0] - lo[F0] * last_f
        out[F0] = lo[F0] * last_l
        out[DN] = hi[DN] - hi[EN] * first_l
        out[EN] = hi[EN] * first_f
        for t in range(TRACERS):
            out[R0 + t] = lo[R0 + t] + lo[F0] * last_r[t]
            out[RN + t] = hi[RN + t] + hi[EN] * first_r[t]
        for part in range(PARTS):
            sent[pl.ds(l * SENT + part, CHIPS, stride=LAYERS * SENT), :] = out[part]
        sent[pl.ds(l * SENT + PARTS, CHIPS, stride=LAYERS * SENT), :] = jnp.zeros((8, 128), F32)
        for k, value in enumerate(last_r + first_r + [last_f, last_l, first_f, first_l]):
            kept[k, l] = value


def pair_part(core, mine, other):
    vmem = pl.BlockSpec(memory_space=pltpu.VMEM)
    return pl.pallas_call(
        pair_kernel,
        in_specs=[pl.BlockSpec(memory_space=pltpu.SMEM), vmem, vmem],
        out_specs=[vmem, vmem],
        out_shape=[
            jax.ShapeDtypeStruct((CHIPS * LAYERS * SENT, 128), F32),
            jax.ShapeDtypeStruct((14, LAYERS, 8, 128), F32),
        ],
        compiler_params=SMALL,
        name="pair_part",
    )(core, mine, other)


def chain_kernel(parts, solved):
    load = lambda chip, part: parts[pl.ds(chip * LAYERS * SENT + part, LAYERS, stride=SENT), :]
    firsts, lasts = [], []
    cd_prev = gate = ratio = reduced = None
    base, known = None, None
    for chip in range(CHIPS):
        d0, f0 = load(chip, D0), load(chip, F0)
        dn, en = load(chip, DN), load(chip, EN)
        r0 = [load(chip, R0 + t) for t in range(TRACERS)]
        rn = [load(chip, RN + t) for t in range(TRACERS)]
        if chip:
            cd0 = load(chip, CD0)
            face = jnp.minimum(cd_prev, cd0)
            down = face + jnp.where(cd_prev > 0.0, load(chip, WA0), 0.0)
            inverse = 1.0 / (base + face)
            ratio = face * inverse
            reduced = [x * inverse for x in known]
            lasts.append((ratio, reduced))
            inverse = 1.0 / (d0 + down * (1.0 - ratio))
            r0 = [x + down * y for x, y in zip(r0, reduced)]
        else:
            inverse = 1.0 / d0
        ahead = f0 * inverse
        here = [x * inverse for x in r0]
        firsts.append((ahead, here))
        base = dn - en * ahead
        known = [x + en * y for x, y in zip(rn, here)]
        cd_prev = load(chip, CDN)
    inverse = 1.0 / base
    last = [x * inverse for x in known]
    for chip in reversed(range(CHIPS)):
        ahead, here = firsts[chip]
        first = [x + ahead * y for x, y in zip(here, last)]
        for t in range(TRACERS):
            solved[pl.ds(chip * LAYERS * BACK + t, LAYERS, stride=BACK), :] = first[t]
            solved[pl.ds(chip * LAYERS * BACK + TRACERS + t, LAYERS, stride=BACK), :] = last[t]
        if chip:
            ratio, reduced = lasts[chip - 1]
            last = [x + ratio * y for x, y in zip(reduced, first)]


def chain_part(parts):
    vmem = pl.BlockSpec(memory_space=pltpu.VMEM)
    return pl.pallas_call(
        chain_kernel,
        in_specs=[vmem],
        out_specs=vmem,
        out_shape=jax.ShapeDtypeStruct((CHIPS * LAYERS * BACK, 128), F32),
        compiler_params=SMALL,
        name="chain_part",
    )(parts)


def middle_kernel(core, solved, kept, mine, theirs):
    first_core = core[0] == 0
    for l in range(LAYERS):
        last_f, last_l, first_f, first_l = (kept[10 + k, l] for k in range(4))
        for t in range(TRACERS):
            first = solved[pl.ds(l * BACK + t, CHIPS, stride=LAYERS * BACK), :]
            last = solved[pl.ds(l * BACK + TRACERS + t, CHIPS, stride=LAYERS * BACK), :]
            before = kept[t, l] + last_f * first + last_l * last
            after = kept[TRACERS + t, l] + first_f * first + first_l * last
            mine[t, l] = jnp.where(first_core, first, after)
            mine[TRACERS + t, l] = jnp.where(first_core, before, last)
            theirs[t, l] = jnp.where(first_core, after, first)
            theirs[TRACERS + t, l] = jnp.where(first_core, last, before)


def middle_part(core, solved, kept):
    vmem = pl.BlockSpec(memory_space=pltpu.VMEM)
    return pl.pallas_call(
        middle_kernel,
        in_specs=[pl.BlockSpec(memory_space=pltpu.SMEM), vmem, vmem],
        out_specs=[vmem, vmem],
        out_shape=[jax.ShapeDtypeStruct((BACK, LAYERS, 8, 128), F32)] * 2,
        compiler_params=SMALL,
        name="middle_part",
    )(core, solved, kept)


def final_kernel(core, red, fill, rho, mine, other, out):
    first_core = core[0] == 0
    for half in range(2):
        pick = (lambda k: jnp.where(first_core, mine[k, 0], other[k, 0])) if half == 0 else (
            lambda k: jnp.where(first_core, other[k, 0], mine[k, 0])
        )
        firsts = [pick(t) for t in range(TRACERS)]
        cells = [pick(TRACERS + t) for t in range(TRACERS)]
        for t in range(TRACERS):
            out[t, 0, line(ROWS - 1, half), :] = cells[t]
            out[t, 0, line(0, half), :] = firsts[t]
        for row in reversed(range(1, ROWS - 1)):
            where = pl.ds((half * ROWS + row) * 8, 8)
            fill_row, rho_row = fill[0, where, :], rho[0, where, :]
            for t in range(TRACERS):
                cells[t] = red[t, 0, where, :] + fill_row * firsts[t] + rho_row * cells[t]
                out[t, 0, line(row, half), :] = cells[t]


def final_part(core, red, fill, rho, mine, other):
    layered = lambda *lead: pl.BlockSpec(lead + (1, 256, 128), lambda l, n=len(lead): (0,) * n + (l, 0, 0))
    packed = pl.BlockSpec((BACK, 1, 8, 128), lambda l: (0, l, 0, 0))
    return pl.pallas_call(
        final_kernel,
        grid=(LAYERS,),
        in_specs=[
            pl.BlockSpec(memory_space=pltpu.SMEM),
            layered(TRACERS),
            layered(),
            layered(),
            packed,
            packed,
        ],
        out_specs=layered(TRACERS),
        out_shape=jax.ShapeDtypeStruct((TRACERS, LAYERS, 256, 128), F32),
        compiler_params=pltpu.CompilerParams(vmem_limit_bytes=12 * 1024 * 1024),
        name="final_part",
    )(core, red, fill, rho, mine, other)


def on_device(tracers, kappa_x, kappa_y, courant, wet_mask, levels):
    count = lax.axis_size("cross")
    core = (lax.axis_index("chan") % 2).astype(jnp.int32).reshape(1)
    pairs = [(i, i ^ 1) for i in range(2 * CHIPS)]
    lines = [[c + 2 * z for z in range(CHIPS)] for c in range(2)]

    lowest, highest = edges(tracers, kappa_y, wet_mask, levels)
    left = lax.ppermute(highest, "cross", [(i, i + 1) for i in range(count - 1)])
    right = lax.ppermute(lowest, "cross", [(i + 1, i) for i in range(count - 1)])
    red, fill, rho, mine, theirs = local_part(
        core,
        folded(tracers),
        folded(kappa_x),
        folded(kappa_y),
        folded(courant),
        folded(wet_mask),
        folded(levels),
        left,
        right,
    )
    other = lax.ppermute(theirs, "chan", pairs)
    sent, kept = pair_part(core, mine, other)
    parts = lax.all_to_all(
        sent.reshape(CHIPS, LAYERS * SENT, 128), "chan", 0, 0, axis_index_groups=lines, tiled=True
    )
    solved = chain_part(parts.reshape(CHIPS * LAYERS * SENT, 128))
    back = lax.all_to_all(
        solved.reshape(CHIPS, LAYERS * BACK, 128), "chan", 0, 0, axis_index_groups=lines, tiled=True
    )
    mine, theirs = middle_part(core, back.reshape(CHIPS * LAYERS * BACK, 128), kept)
    other = lax.ppermute(theirs, "chan", pairs)
    return unfolded(final_part(core, red, fill, rho, mine, other))


def solution(mesh):
    placed = (
        P(None, None, "chan", "cross"),
        P(None, "chan", "cross"),
        P(None, "chan", "cross"),
        P(None, "chan", "cross"),
        P("chan", "cross"),
        P("chan", "cross"),
    )
    return jax.shard_map(
        on_device,
        mesh=mesh,
        in_specs=placed,
        out_specs=P(None, None, "chan", "cross"),
        check_vma=False,
    )
```

```python
import functools

import jax
import jax.numpy as jnp
from jax import lax
from jax.experimental import pallas as pl
from jax.experimental.pallas import tpu as pltpu
from jax.sharding import PartitionSpec as P

TRACERS = 5
LAYERS = 4
ROWS = 16
CHIPS = 8
CD0, WA0, D0, F0, R0, CDN, DN, EN, RN = 0, 1, 2, 3, 4, 9, 10, 11, 12
PARTS = 17
SENT = 18
BACK = 10
F32 = jnp.float32
SMALL = pltpu.CompilerParams(vmem_limit_bytes=4 * 1024 * 1024)


def folded(cells):
    lead = cells.shape[:-2]
    cells = cells.reshape(lead + (2, 8, 16, 128))
    return jnp.swapaxes(cells, len(lead) + 1, len(lead) + 2).reshape(lead + (256, 128))


def unfolded(cells):
    lead = cells.shape[:-2]
    cells = cells.reshape(lead + (2, 16, 8, 128))
    return jnp.swapaxes(cells, len(lead) + 1, len(lead) + 2).reshape(lead + (16, 2048))


def line(row, half):
    return pl.ds((row // 8) * 128 + half * 64 + row % 8, 8, stride=8)


def tile(row_tile, column_tile):
    return pl.ds(row_tile * 128 + column_tile * 8, 8)


def edges_kernel(tr_lo, tr_hi, ky_lo, ky_hi, wet_lo, wet_hi, lev_lo, lev_hi, out_lo, out_hi):
    lane = lax.broadcasted_iota(jnp.int32, (8, 128), 1)
    for tr, ky, wet, lev, out, at in (
        (tr_lo, ky_lo, wet_lo, lev_lo, out_lo, 0),
        (tr_hi, ky_hi, wet_hi, lev_hi, out_hi, 127),
    ):
        for l in range(LAYERS):
            for i in range(2):
                rows = pl.ds(i * 8, 8)
                active = (wet[rows, :] > 0) & (lev[rows, :] > l)
                cross = jnp.where(active, ky[l, rows, :], 0.0)
                packed = jnp.where(lane < 64, 0.0, jnp.broadcast_to(cross[:, at : at + 1], (8, 128)))
                for t in range(TRACERS):
                    packed = jnp.where(lane == t, pltpu.roll(tr[t, l, rows, :], (t - at) % 128, 1), packed)
                out[l, rows, :] = packed


def edges(tracers, kappa_y, wet, levels):
    def spec(lead, at):
        zeros = (0,) * (len(lead) + 1)
        return pl.BlockSpec(lead + (16, 128), lambda i, zeros=zeros, at=at: zeros + (at,))

    return pl.pallas_call(
        edges_kernel,
        grid=(1,),
        in_specs=[
            spec((TRACERS, LAYERS), 0),
            spec((TRACERS, LAYERS), 15),
            spec((LAYERS,), 0),
            spec((LAYERS,), 15),
            spec((), 0),
            spec((), 15),
            spec((), 0),
            spec((), 15),
        ],
        out_specs=[pl.BlockSpec((LAYERS, 16, 128), lambda i: (0, 0, 0))] * 2,
        out_shape=[jax.ShapeDtypeStruct((LAYERS, 16, 128), F32)] * 2,
        compiler_params=SMALL,
        name="edges",
    )(*(pltpu.with_memory_space_constraint(x, pltpu.HBM) for x in (tracers, tracers, kappa_y, kappa_y, wet, wet, levels, levels)))


def local_kernel(
    core, tr, kx, ky, co, wet, lev, red, fill, rho, inv, gain, mine, theirs, side
):
    lax.fori_loop(
        0,
        LAYERS,
        lambda layer, none: local_layer(
            layer, core, tr, kx, ky, co, wet, lev, red, fill, rho, inv, gain, mine, theirs, side
        ),
        None,
    )


def local_layer(
    layer, core, tr, kx, ky, co, wet, lev, red, fill, rho, inv, gain, mine, theirs, side
):
    first_core = core[0] == 0
    lane = lax.broadcasted_iota(jnp.int32, (8, 128), 1)
    head, tail = lane == 0, lane == 127

    for i in range(2):

        def cross_of(j):
            active = (wet[tile(i, j), :] > 0) & (lev[tile(i, j), :] > layer)
            return jnp.where(active, ky[layer, tile(i, j), :], 0.0)

        def ahead(now, following):
            return jnp.where(tail, pltpu.roll(following, 127, 1), pltpu.roll(now, 127, 1))

        faces = []
        now = cross_of(0)
        for j in range(16):
            if j < 15:
                following = cross_of(j + 1)
                faces.append(jnp.minimum(now, ahead(now, following)))
                now = following
            else:
                faces.append(jnp.where(tail, 0.0, jnp.minimum(now, pltpu.roll(now, 127, 1))))
        for t in range(TRACERS):
            now = tr[t, layer, tile(i, 0), :]
            shifted = pltpu.roll(now, 127, 1)
            before = jnp.zeros((8, 128), F32)
            for j in range(16):
                if j < 15:
                    following = tr[t, layer, tile(i, j + 1), :]
                    shifted_following = pltpu.roll(following, 127, 1)
                    flux = faces[j] * (jnp.where(tail, shifted_following, shifted) - now)
                else:
                    flux = faces[j] * (shifted - now)
                behind = pltpu.roll(flux, 1, 1)
                side[t, tile(i, j), :] = now + flux - jnp.where(head, before, behind)
                before = behind
                now, shifted = following, shifted_following

    halves = []
    for half in range(2):

        def load(row):
            where = line(row, half)
            active = (wet[where, :] > 0) & (lev[where, :] > layer)
            act = jnp.where(active, 1.0, 0.0).astype(F32)
            return act, kx[layer, where, :] * act, co[layer, where, :]

        out = [None] * PARTS
        act_prev, cd_prev, co_prev = load(0)
        act, cd, cour = load(1)
        out[CD0] = cd_prev
        out[WA0] = act_prev * co_prev
        face_first = jnp.minimum(cd_prev, cd)
        face_down = face_first
        rho_row = None
        for row in range(1, ROWS - 1):
            act_next, cd_next, co_next = load(row + 1)
            face_up = jnp.minimum(cd, cd_next)
            low = act * (face_down + cour * act_prev)
            where = pl.ds((half * ROWS + row) * 8, 8)
            if row == 1:
                inverse = 1.0 / (1.0 + face_up + low)
                rho_row = face_up * inverse
                gain_row = low * inverse
                fill_row = gain_row
                reds = [side[t, line(row, half), :] * inverse for t in range(TRACERS)]
                sums = list(reds)
                sum_fill = fill_row
                chain = rho_row
            else:
                inverse = 1.0 / (1.0 + face_up + low * (1.0 - rho_row))
                rho_row = face_up * inverse
                gain_row = low * inverse
                fill_row = gain_row * fill_row
                reds = [side[t, line(row, half), :] * inverse + gain_row * reds[t] for t in range(TRACERS)]
                sums = [sums[t] + chain * reds[t] for t in range(TRACERS)]
                sum_fill = sum_fill + chain * fill_row
                chain = chain * rho_row
            rho[layer, where, :] = rho_row
            fill[layer, where, :] = fill_row
            inv[layer, where, :] = inverse
            gain[layer, where, :] = gain_row
            for t in range(TRACERS):
                red[t, layer, where, :] = reds[t]
            act_prev = act
            act, cd, cour = act_next, cd_next, co_next
            face_down = face_up
        low = act * (face_down + cour * act_prev)
        gain[layer, pl.ds(half * ROWS * 8, 8), :] = face_first
        gain[layer, pl.ds((half * ROWS + ROWS - 1) * 8, 8), :] = low
        out[D0] = 1.0 + face_first * (1.0 - sum_fill)
        out[F0] = face_first * chain
        out[CDN] = cd
        out[DN] = 1.0 + low * (1.0 - rho_row)
        out[EN] = low * fill_row
        for t in range(TRACERS):
            out[R0 + t] = side[t, line(0, half), :] + face_first * sums[t]
            out[RN + t] = side[t, line(ROWS - 1, half), :] + low * reds[t]
        halves.append(out)
    for part in range(PARTS):
        mine[part, layer] = jnp.where(first_core, halves[0][part], halves[1][part])
        theirs[part, layer] = jnp.where(first_core, halves[1][part], halves[0][part])


def local_part(core, tracers, kappa_x, kappa_y, courant, wet, levels):
    vmem = pl.BlockSpec(memory_space=pltpu.VMEM)
    return pl.pallas_call(
        local_kernel,
        in_specs=[pl.BlockSpec(memory_space=pltpu.SMEM)] + [vmem] * 6,
        out_specs=[vmem] * 7,
        out_shape=[
            jax.ShapeDtypeStruct((TRACERS, LAYERS, 256, 128), F32),
            jax.ShapeDtypeStruct((LAYERS, 256, 128), F32),
            jax.ShapeDtypeStruct((LAYERS, 256, 128), F32),
            jax.ShapeDtypeStruct((LAYERS, 256, 128), F32),
            jax.ShapeDtypeStruct((LAYERS, 256, 128), F32),
            jax.ShapeDtypeStruct((PARTS, LAYERS, 8, 128), F32),
            jax.ShapeDtypeStruct((PARTS, LAYERS, 8, 128), F32),
        ],
        scratch_shapes=[pltpu.VMEM((TRACERS, 256, 128), F32)],
        compiler_params=pltpu.CompilerParams(vmem_limit_bytes=12 * 1024 * 1024),
        name="local_part",
    )(core, tracers, kappa_x, kappa_y, courant, wet, levels)


def outer_kernel(
    where_am_i, own_lo, own_hi, left, right, inv, gain, rho, mine_in, theirs_in, mine, theirs, fix_lo, fix_hi
):
    mine[...] = mine_in[...]
    theirs[...] = theirs_in[...]
    lane = lax.broadcasted_iota(jnp.int32, (LAYERS, 128), 1)
    for e, (own, halo, fix) in enumerate(((own_lo, left, fix_lo), (own_hi, right, fix_hi))):
        at, sub = (0, 0) if e == 0 else (127, 7)
        inside = where_am_i[1 + e] > 0

        def coefficient(ref, row):
            values = ref[pl.ds((e * ROWS + row) * 8 + sub, LAYERS, stride=256), :]
            return jnp.broadcast_to(values[:, at : at + 1], (LAYERS, 128))

        deltas = []
        for row in range(ROWS):
            here = own[pl.ds(row, LAYERS, stride=ROWS), :]
            there = jnp.where(inside, halo[pl.ds(row, LAYERS, stride=ROWS), :], 0.0)
            face = pltpu.roll(jnp.minimum(here, there), 64, 1)
            deltas.append(face * (there - here))
        rhos = [None] + [coefficient(rho, row) for row in range(1, ROWS - 1)]
        reds = [None] * ROWS
        for row in range(1, ROWS - 1):
            reds[row] = deltas[row] * coefficient(inv, row)
            if row == 1:
                total, chain = reds[1], rhos[1]
            else:
                reds[row] = reds[row] + coefficient(gain, row) * reds[row - 1]
                total = total + chain * reds[row]
                chain = chain * rhos[row]
        first = deltas[0] + coefficient(gain, 0) * total
        last = deltas[ROWS - 1] + coefficient(gain, ROWS - 1) * reds[ROWS - 2]
        zero = jnp.zeros((LAYERS, 128), F32)
        fix[pl.ds(0, LAYERS, stride=ROWS), :] = zero
        fix[pl.ds(ROWS - 1, LAYERS, stride=ROWS), :] = zero
        value = zero
        for row in reversed(range(1, ROWS - 1)):
            value = reds[row] + rhos[row] * value
            fix[pl.ds(row, LAYERS, stride=ROWS), :] = value

        def add_to(ref):
            for t in range(TRACERS):
                for part, change in ((R0 + t, first), (RN + t, last)):
                    rows = pl.ds(part * LAYERS * 8 + sub, LAYERS, stride=8)
                    ref[rows, :] = ref[rows, :] + jnp.where(lane == at, pltpu.roll(change, (at - t) % 128, 1), 0.0)

        pl.when(where_am_i[0] == e)(lambda: add_to(mine))
        pl.when(where_am_i[0] != e)(lambda: add_to(theirs))


def outer_part(where_am_i, own_lo, own_hi, left, right, inv, gain, rho, mine, theirs):
    vmem = pl.BlockSpec(memory_space=pltpu.VMEM)
    flat = lambda x: x.reshape(-1, 128)
    mine, theirs, fix_lo, fix_hi = pl.pallas_call(
        outer_kernel,
        in_specs=[pl.BlockSpec(memory_space=pltpu.SMEM)] + [vmem] * 9,
        out_specs=[vmem] * 4,
        out_shape=[jax.ShapeDtypeStruct((PARTS * LAYERS * 8, 128), F32)] * 2
        + [jax.ShapeDtypeStruct((LAYERS * ROWS, 128), F32)] * 2,
        compiler_params=SMALL,
        name="outer_part",
    )(where_am_i, *(flat(x) for x in (own_lo, own_hi, left, right, inv, gain, rho, mine, theirs)))
    packed = (PARTS, LAYERS, 8, 128)
    return mine.reshape(packed), theirs.reshape(packed), fix_lo, fix_hi


def pair_kernel(core, mine, other, sent, kept):
    first_core = core[0] == 0
    for l in range(LAYERS):
        a = [mine[part, l] for part in range(PARTS)]
        b = [other[part, l] for part in range(PARTS)]
        lo = [jnp.where(first_core, x, y) for x, y in zip(a, b)]
        hi = [jnp.where(first_core, y, x) for x, y in zip(a, b)]
        face = jnp.minimum(lo[CDN], hi[CD0])
        down = face + jnp.where(lo[CDN] > 0.0, hi[WA0], 0.0)
        scale = 1.0 / (lo[DN] * (hi[D0] + down) + face * hi[D0])
        in_b = scale * (hi[D0] + down)
        in_g = scale * face
        in_w = scale * down
        in_a = scale * (lo[DN] + face)
        last_f, last_l = in_b * lo[EN], in_g * hi[F0]
        first_f, first_l = in_w * lo[EN], in_a * hi[F0]
        last_r = [in_b * lo[RN + t] + in_g * hi[R0 + t] for t in range(TRACERS)]
        first_r = [in_w * lo[RN + t] + in_a * hi[R0 + t] for t in range(TRACERS)]
        out = [None] * PARTS
        out[CD0], out[WA0], out[CDN] = lo[CD0], lo[WA0], hi[CDN]
        out[D0] = lo[D0] - lo[F0] * last_f
        out[F0] = lo[F0] * last_l
        out[DN] = hi[DN] - hi[EN] * first_l
        out[EN] = hi[EN] * first_f
        for t in range(TRACERS):
            out[R0 + t] = lo[R0 + t] + lo[F0] * last_r[t]
            out[RN + t] = hi[RN + t] + hi[EN] * first_r[t]
        for part in range(PARTS):
            sent[pl.ds(l * SENT + part, CHIPS, stride=LAYERS * SENT), :] = out[part]
        sent[pl.ds(l * SENT + PARTS, CHIPS, stride=LAYERS * SENT), :] = jnp.zeros((8, 128), F32)
        for k, value in enumerate(last_r + first_r + [last_f, last_l, first_f, first_l]):
            kept[k, l] = value


def pair_part(core, mine, other):
    vmem = pl.BlockSpec(memory_space=pltpu.VMEM)
    return pl.pallas_call(
        pair_kernel,
        in_specs=[pl.BlockSpec(memory_space=pltpu.SMEM), vmem, vmem],
        out_specs=[vmem, vmem],
        out_shape=[
            jax.ShapeDtypeStruct((CHIPS * LAYERS * SENT, 128), F32),
            jax.ShapeDtypeStruct((14, LAYERS, 8, 128), F32),
        ],
        compiler_params=SMALL,
        name="pair_part",
    )(core, mine, other)


def chain_kernel(parts, solved):
    load = lambda chip, part: parts[pl.ds(chip * LAYERS * SENT + part, LAYERS, stride=SENT), :]
    firsts, lasts = [], []
    cd_prev = gate = ratio = reduced = None
    base, known = None, None
    for chip in range(CHIPS):
        d0, f0 = load(chip, D0), load(chip, F0)
        dn, en = load(chip, DN), load(chip, EN)
        r0 = [load(chip, R0 + t) for t in range(TRACERS)]
        rn = [load(chip, RN + t) for t in range(TRACERS)]
        if chip:
            cd0 = load(chip, CD0)
            face = jnp.minimum(cd_prev, cd0)
            down = face + jnp.where(cd_prev > 0.0, load(chip, WA0), 0.0)
            inverse = 1.0 / (base + face)
            ratio = face * inverse
            reduced = [x * inverse for x in known]
            lasts.append((ratio, reduced))
            inverse = 1.0 / (d0 + down * (1.0 - ratio))
            r0 = [x + down * y for x, y in zip(r0, reduced)]
        else:
            inverse = 1.0 / d0
        ahead = f0 * inverse
        here = [x * inverse for x in r0]
        firsts.append((ahead, here))
        base = dn - en * ahead
        known = [x + en * y for x, y in zip(rn, here)]
        cd_prev = load(chip, CDN)
    inverse = 1.0 / base
    last = [x * inverse for x in known]
    for chip in reversed(range(CHIPS)):
        ahead, here = firsts[chip]
        first = [x + ahead * y for x, y in zip(here, last)]
        for t in range(TRACERS):
            solved[pl.ds(chip * LAYERS * BACK + t, LAYERS, stride=BACK), :] = first[t]
            solved[pl.ds(chip * LAYERS * BACK + TRACERS + t, LAYERS, stride=BACK), :] = last[t]
        if chip:
            ratio, reduced = lasts[chip - 1]
            last = [x + ratio * y for x, y in zip(reduced, first)]


def chain_part(parts):
    vmem = pl.BlockSpec(memory_space=pltpu.VMEM)
    return pl.pallas_call(
        chain_kernel,
        in_specs=[vmem],
        out_specs=vmem,
        out_shape=jax.ShapeDtypeStruct((CHIPS * LAYERS * BACK, 128), F32),
        compiler_params=SMALL,
        name="chain_part",
    )(parts)


def middle_kernel(core, solved, kept, mine, theirs):
    first_core = core[0] == 0
    for l in range(LAYERS):
        last_f, last_l, first_f, first_l = (kept[10 + k, l] for k in range(4))
        for t in range(TRACERS):
            first = solved[pl.ds(l * BACK + t, CHIPS, stride=LAYERS * BACK), :]
            last = solved[pl.ds(l * BACK + TRACERS + t, CHIPS, stride=LAYERS * BACK), :]
            before = kept[t, l] + last_f * first + last_l * last
            after = kept[TRACERS + t, l] + first_f * first + first_l * last
            mine[t, l] = jnp.where(first_core, first, after)
            mine[TRACERS + t, l] = jnp.where(first_core, before, last)
            theirs[t, l] = jnp.where(first_core, after, first)
            theirs[TRACERS + t, l] = jnp.where(first_core, last, before)


def middle_part(core, solved, kept):
    vmem = pl.BlockSpec(memory_space=pltpu.VMEM)
    return pl.pallas_call(
        middle_kernel,
        in_specs=[pl.BlockSpec(memory_space=pltpu.SMEM), vmem, vmem],
        out_specs=[vmem, vmem],
        out_shape=[jax.ShapeDtypeStruct((BACK, LAYERS, 8, 128), F32)] * 2,
        compiler_params=SMALL,
        name="middle_part",
    )(core, solved, kept)


def final_kernel(core, red, fill, rho, mine, other, fix_lo, fix_hi, out):
    first_core = core[0] == 0
    for half in range(2):
        pick = (lambda k: jnp.where(first_core, mine[k, 0], other[k, 0])) if half == 0 else (
            lambda k: jnp.where(first_core, other[k, 0], mine[k, 0])
        )
        firsts = [pick(t) for t in range(TRACERS)]
        cells = [pick(TRACERS + t) for t in range(TRACERS)]
        for t in range(TRACERS):
            out[t, 0, line(ROWS - 1, half), :] = cells[t]
            out[t, 0, line(0, half), :] = firsts[t]
        for row in reversed(range(1, ROWS - 1)):
            where = pl.ds((half * ROWS + row) * 8, 8)
            fill_row, rho_row = fill[0, where, :], rho[0, where, :]
            for t in range(TRACERS):
                cells[t] = red[t, 0, where, :] + fill_row * firsts[t] + rho_row * cells[t]
                out[t, 0, line(row, half), :] = cells[t]
    lane = lax.broadcasted_iota(jnp.int32, (8, 128), 1)
    for i in range(2):
        for fix, at, column in ((fix_lo, 0, 0), (fix_hi, 127, 15)):
            change = fix[pl.ds(i * 8, 8), :]
            for t in range(TRACERS):
                where = tile(i, column)
                moved = jnp.where(lane == at, pltpu.roll(change, (at - t) % 128, 1), 0.0)
                out[t, 0, where, :] = out[t, 0, where, :] + moved


def final_part(core, red, fill, rho, mine, other, fix_lo, fix_hi):
    layered = lambda *lead: pl.BlockSpec(lead + (1, 256, 128), lambda l, n=len(lead): (0,) * n + (l, 0, 0))
    packed = pl.BlockSpec((BACK, 1, 8, 128), lambda l: (0, l, 0, 0))
    return pl.pallas_call(
        final_kernel,
        grid=(LAYERS,),
        in_specs=[
            pl.BlockSpec(memory_space=pltpu.SMEM),
            layered(TRACERS),
            layered(),
            layered(),
            packed,
            packed,
            pl.BlockSpec((ROWS, 128), lambda l: (l, 0)),
            pl.BlockSpec((ROWS, 128), lambda l: (l, 0)),
        ],
        out_specs=layered(TRACERS),
        out_shape=jax.ShapeDtypeStruct((TRACERS, LAYERS, 256, 128), F32),
        compiler_params=pltpu.CompilerParams(vmem_limit_bytes=12 * 1024 * 1024),
        name="final_part",
    )(core, red, fill, rho, mine, other, fix_lo, fix_hi)


def on_device(tracers, kappa_x, kappa_y, courant, wet_mask, levels):
    count = lax.axis_size("cross")
    along, across = lax.axis_index("chan"), lax.axis_index("cross")
    core = jnp.stack([along % 2, across > 0, across < count - 1]).astype(jnp.int32)
    pairs = [(i, i ^ 1) for i in range(2 * CHIPS)]
    lines = [[c + 2 * z for z in range(CHIPS)] for c in range(2)]

    lowest, highest = edges(tracers, kappa_y, wet_mask, levels)
    left = lax.ppermute(highest, "cross", [(i, (i + 1) % count) for i in range(count)])
    right = lax.ppermute(lowest, "cross", [((i + 1) % count, i) for i in range(count)])
    red, fill, rho, inv, gain, mine, theirs = local_part(
        core,
        folded(tracers),
        folded(kappa_x),
        folded(kappa_y),
        folded(courant),
        folded(wet_mask),
        folded(levels),
    )
    mine, theirs, fix_lo, fix_hi = outer_part(
        core, lowest, highest, left, right, inv, gain, rho, mine, theirs
    )
    other = lax.ppermute(theirs, "chan", pairs)
    sent, kept = pair_part(core, mine, other)
    parts = lax.all_to_all(
        sent.reshape(CHIPS, LAYERS * SENT, 128), "chan", 0, 0, axis_index_groups=lines, tiled=True
    )
    solved = chain_part(parts.reshape(CHIPS * LAYERS * SENT, 128))
    back = lax.all_to_all(
        solved.reshape(CHIPS, LAYERS * BACK, 128), "chan", 0, 0, axis_index_groups=lines, tiled=True
    )
    mine, theirs = middle_part(core, back.reshape(CHIPS * LAYERS * BACK, 128), kept)
    other = lax.ppermute(theirs, "chan", pairs)
    return unfolded(final_part(core, red, fill, rho, mine, other, fix_lo, fix_hi))


def solution(mesh):
    placed = (
        P(None, None, "chan", "cross"),
        P(None, "chan", "cross"),
        P(None, "chan", "cross"),
        P(None, "chan", "cross"),
        P("chan", "cross"),
        P("chan", "cross"),
    )
    return jax.shard_map(
        on_device,
        mesh=mesh,
        in_specs=placed,
        out_specs=P(None, None, "chan", "cross"),
        check_vma=False,
    )
```

```python
import functools

import jax
import jax.numpy as jnp
from jax import lax
from jax.experimental import pallas as pl
from jax.experimental.pallas import tpu as pltpu
from jax.sharding import PartitionSpec as P

TRACERS = 5
LAYERS = 4
ROWS = 16
CHIPS = 8
CD0, WA0, D0, F0, R0, CDN, DN, EN, RN = 0, 1, 2, 3, 4, 9, 10, 11, 12
PARTS = 17
SENT = 18
BACK = 10
F32 = jnp.float32
SMALL = pltpu.CompilerParams(vmem_limit_bytes=4 * 1024 * 1024)


def folded(cells):
    lead = cells.shape[:-2]
    cells = cells.reshape(lead + (2, 8, 16, 128))
    return jnp.swapaxes(cells, len(lead) + 1, len(lead) + 2).reshape(lead + (256, 128))


def unfolded(cells):
    lead = cells.shape[:-2]
    cells = cells.reshape(lead + (2, 16, 8, 128))
    return jnp.swapaxes(cells, len(lead) + 1, len(lead) + 2).reshape(lead + (16, 2048))


def in_hbm(cells):
    return pltpu.with_memory_space_constraint(cells, pltpu.HBM)


def line(row, half):
    return pl.ds((row // 8) * 128 + half * 64 + row % 8, 8, stride=8)


def is_first_core():
    return lax.axis_index("chan") % 2 == 0


def tile(row_tile, column_tile):
    return pl.ds(row_tile * 128 + column_tile * 8, 8)


def edges_kernel(tr_lo, tr_hi, ky_lo, ky_hi, wet_lo, wet_hi, lev_lo, lev_hi, out_lo, out_hi):
    lane = lax.broadcasted_iota(jnp.int32, (8, 128), 1)
    for tr, ky, wet, lev, out, at in (
        (tr_lo, ky_lo, wet_lo, lev_lo, out_lo, 0),
        (tr_hi, ky_hi, wet_hi, lev_hi, out_hi, 127),
    ):
        for l in range(LAYERS):
            for i in range(2):
                rows = pl.ds(i * 8, 8)
                active = (wet[rows, :] > 0) & (lev[rows, :] > l)
                cross = jnp.where(active, ky[l, rows, :], 0.0)
                packed = jnp.where(lane < 64, 0.0, jnp.broadcast_to(cross[:, at : at + 1], (8, 128)))
                for t in range(TRACERS):
                    packed = jnp.where(lane == t, pltpu.roll(tr[t, l, rows, :], (t - at) % 128, 1), packed)
                out[l, rows, :] = packed


def edges(tracers, kappa_y, wet, levels):
    def spec(lead, at):
        zeros = (0,) * (len(lead) + 1)
        return pl.BlockSpec(lead + (16, 128), lambda i, zeros=zeros, at=at: zeros + (at,))

    return pl.pallas_call(
        edges_kernel,
        grid=(1,),
        in_specs=[
            spec((TRACERS, LAYERS), 0),
            spec((TRACERS, LAYERS), 15),
            spec((LAYERS,), 0),
            spec((LAYERS,), 15),
            spec((), 0),
            spec((), 15),
            spec((), 0),
            spec((), 15),
        ],
        out_specs=[pl.BlockSpec((LAYERS, 16, 128), lambda i: (0, 0, 0))] * 2,
        out_shape=[jax.ShapeDtypeStruct((LAYERS, 16, 128), F32)] * 2,
        compiler_params=SMALL,
        name="edges",
    )(*(in_hbm(x) for x in (tracers, tracers, kappa_y, kappa_y, wet, wet, levels, levels)))


def local_kernel(
    tr, kx_hbm, ky, co_hbm, wet, lev, red, fill, rho, inv, gain, mine, theirs, side, kx, co, sems
):
    copies = [
        pltpu.make_async_copy(kx_hbm, kx, sems.at[0]),
        pltpu.make_async_copy(co_hbm, co, sems.at[1]),
    ]
    for copy in copies:
        copy.start()
    def one(layer, none):
        right_sides(layer, tr, ky, wet, lev, side)

        @pl.when(layer == 0)
        def _():
            for copy in copies:
                copy.wait()

        eliminate(layer, kx, co, wet, lev, red, fill, rho, inv, gain, mine, theirs, side)

    lax.fori_loop(0, LAYERS, one, None)


def right_sides(layer, tr, ky, wet, lev, side):
    lane = lax.broadcasted_iota(jnp.int32, (8, 128), 1)
    head, tail = lane == 0, lane == 127

    for i in range(2):

        def cross_of(j):
            active = (wet[tile(i, j), :] > 0) & (lev[tile(i, j), :] > layer)
            return jnp.where(active, ky[layer, tile(i, j), :], 0.0)

        def ahead(now, following):
            return jnp.where(tail, pltpu.roll(following, 127, 1), pltpu.roll(now, 127, 1))

        faces = []
        now = cross_of(0)
        for j in range(16):
            if j < 15:
                following = cross_of(j + 1)
                faces.append(jnp.minimum(now, ahead(now, following)))
                now = following
            else:
                faces.append(jnp.where(tail, 0.0, jnp.minimum(now, pltpu.roll(now, 127, 1))))
        for t in range(TRACERS):
            now = tr[t, layer, tile(i, 0), :]
            shifted = pltpu.roll(now, 127, 1)
            before = jnp.zeros((8, 128), F32)
            for j in range(16):
                if j < 15:
                    following = tr[t, layer, tile(i, j + 1), :]
                    shifted_following = pltpu.roll(following, 127, 1)
                    flux = faces[j] * (jnp.where(tail, shifted_following, shifted) - now)
                else:
                    flux = faces[j] * (shifted - now)
                behind = pltpu.roll(flux, 1, 1)
                side[t, tile(i, j), :] = now + flux - jnp.where(head, before, behind)
                before = behind
                now, shifted = following, shifted_following


def eliminate(layer, kx, co, wet, lev, red, fill, rho, inv, gain, mine, theirs, side):
    first_core = is_first_core()
    halves = []
    for half in range(2):

        def load(row):
            where = line(row, half)
            active = (wet[where, :] > 0) & (lev[where, :] > layer)
            act = jnp.where(active, 1.0, 0.0).astype(F32)
            return act, kx[layer, where, :] * act, co[layer, where, :]

        out = [None] * PARTS
        act_prev, cd_prev, co_prev = load(0)
        act, cd, cour = load(1)
        out[CD0] = cd_prev
        out[WA0] = act_prev * co_prev
        face_first = jnp.minimum(cd_prev, cd)
        face_down = face_first
        rho_row = None
        for row in range(1, ROWS - 1):
            act_next, cd_next, co_next = load(row + 1)
            face_up = jnp.minimum(cd, cd_next)
            low = act * (face_down + cour * act_prev)
            where = pl.ds((half * ROWS + row) * 8, 8)
            if row == 1:
                inverse = 1.0 / (1.0 + face_up + low)
                rho_row = face_up * inverse
                gain_row = low * inverse
                fill_row = gain_row
                reds = [side[t, line(row, half), :] * inverse for t in range(TRACERS)]
                sums = list(reds)
                sum_fill = fill_row
                chain = rho_row
            else:
                inverse = 1.0 / (1.0 + face_up + low * (1.0 - rho_row))
                rho_row = face_up * inverse
                gain_row = low * inverse
                fill_row = gain_row * fill_row
                reds = [side[t, line(row, half), :] * inverse + gain_row * reds[t] for t in range(TRACERS)]
                sums = [sums[t] + chain * reds[t] for t in range(TRACERS)]
                sum_fill = sum_fill + chain * fill_row
                chain = chain * rho_row
            rho[layer, where, :] = rho_row
            fill[layer, where, :] = fill_row
            inv[layer, where, :] = inverse
            gain[layer, where, :] = gain_row
            for t in range(TRACERS):
                red[t, layer, where, :] = reds[t]
            act_prev = act
            act, cd, cour = act_next, cd_next, co_next
            face_down = face_up
        low = act * (face_down + cour * act_prev)
        gain[layer, pl.ds(half * ROWS * 8, 8), :] = face_first
        gain[layer, pl.ds((half * ROWS + ROWS - 1) * 8, 8), :] = low
        out[D0] = 1.0 + face_first * (1.0 - sum_fill)
        out[F0] = face_first * chain
        out[CDN] = cd
        out[DN] = 1.0 + low * (1.0 - rho_row)
        out[EN] = low * fill_row
        for t in range(TRACERS):
            out[R0 + t] = side[t, line(0, half), :] + face_first * sums[t]
            out[RN + t] = side[t, line(ROWS - 1, half), :] + low * reds[t]
        halves.append(out)
    for part in range(PARTS):
        mine[part, layer] = jnp.where(first_core, halves[0][part], halves[1][part])
        theirs[part, layer] = jnp.where(first_core, halves[1][part], halves[0][part])


def local_part(tracers, kappa_x, kappa_y, courant, wet, levels):
    vmem = pl.BlockSpec(memory_space=pltpu.VMEM)
    hbm = pl.BlockSpec(memory_space=pltpu.HBM)
    layered = jax.ShapeDtypeStruct((LAYERS, 256, 128), F32)
    packed = jax.ShapeDtypeStruct((PARTS, LAYERS, 8, 128), F32)
    return pl.pallas_call(
        local_kernel,
        in_specs=[vmem, hbm, vmem, hbm, vmem, vmem],
        out_specs=[vmem] * 7,
        out_shape=[jax.ShapeDtypeStruct((TRACERS, LAYERS, 256, 128), F32)] + [layered] * 4 + [packed] * 2,
        scratch_shapes=[
            pltpu.VMEM((TRACERS, 256, 128), F32),
            pltpu.VMEM((LAYERS, 256, 128), F32),
            pltpu.VMEM((LAYERS, 256, 128), F32),
            pltpu.SemaphoreType.DMA((2,)),
        ],
        compiler_params=pltpu.CompilerParams(vmem_limit_bytes=12 * 1024 * 1024),
        name="local_part",
    )(tracers, in_hbm(kappa_x), kappa_y, in_hbm(courant), wet, levels)


def outer_kernel(
    own_lo, own_hi, left, right, inv, gain, rho, mine_in, theirs_in, mine, theirs, fix_lo, fix_hi
):
    place = lax.axis_index("cross")
    first_core = is_first_core()
    mine[...] = mine_in[...]
    theirs[...] = theirs_in[...]
    lane = lax.broadcasted_iota(jnp.int32, (LAYERS, 128), 1)
    for e, (own, halo, fix) in enumerate(((own_lo, left, fix_lo), (own_hi, right, fix_hi))):
        at, sub = (0, 0) if e == 0 else (127, 7)
        inside = (place > 0) if e == 0 else (place < lax.axis_size("cross") - 1)

        def coefficient(ref, row):
            values = ref[pl.ds((e * ROWS + row) * 8 + sub, LAYERS, stride=256), :]
            return jnp.broadcast_to(values[:, at : at + 1], (LAYERS, 128))

        deltas = []
        for row in range(ROWS):
            here = own[pl.ds(row, LAYERS, stride=ROWS), :]
            there = jnp.where(inside, halo[pl.ds(row, LAYERS, stride=ROWS), :], 0.0)
            face = pltpu.roll(jnp.minimum(here, there), 64, 1)
            deltas.append(face * (there - here))
        rhos = [None] + [coefficient(rho, row) for row in range(1, ROWS - 1)]
        reds = [None] * ROWS
        for row in range(1, ROWS - 1):
            reds[row] = deltas[row] * coefficient(inv, row)
            if row == 1:
                total, chain = reds[1], rhos[1]
            else:
                reds[row] = reds[row] + coefficient(gain, row) * reds[row - 1]
                total = total + chain * reds[row]
                chain = chain * rhos[row]
        first = deltas[0] + coefficient(gain, 0) * total
        last = deltas[ROWS - 1] + coefficient(gain, ROWS - 1) * reds[ROWS - 2]
        zero = jnp.zeros((LAYERS, 128), F32)
        fix[pl.ds(0, LAYERS, stride=ROWS), :] = zero
        fix[pl.ds(ROWS - 1, LAYERS, stride=ROWS), :] = zero
        value = zero
        for row in reversed(range(1, ROWS - 1)):
            value = reds[row] + rhos[row] * value
            fix[pl.ds(row, LAYERS, stride=ROWS), :] = value

        def add_to(ref):
            for t in range(TRACERS):
                for part, change in ((R0 + t, first), (RN + t, last)):
                    rows = pl.ds(part * LAYERS * 8 + sub, LAYERS, stride=8)
                    ref[rows, :] = ref[rows, :] + jnp.where(lane == at, pltpu.roll(change, (at - t) % 128, 1), 0.0)

        pl.when(first_core if e == 0 else jnp.logical_not(first_core))(lambda: add_to(mine))
        pl.when(jnp.logical_not(first_core) if e == 0 else first_core)(lambda: add_to(theirs))


def outer_part(own_lo, own_hi, left, right, inv, gain, rho, mine, theirs):
    vmem = pl.BlockSpec(memory_space=pltpu.VMEM)
    flat = lambda x: x.reshape(-1, 128)
    mine, theirs, fix_lo, fix_hi = pl.pallas_call(
        outer_kernel,
        in_specs=[vmem] * 9,
        out_specs=[vmem] * 4,
        out_shape=[jax.ShapeDtypeStruct((PARTS * LAYERS * 8, 128), F32)] * 2
        + [jax.ShapeDtypeStruct((LAYERS * ROWS, 128), F32)] * 2,
        compiler_params=SMALL,
        name="outer_part",
    )(*(flat(x) for x in (own_lo, own_hi, left, right, inv, gain, rho, mine, theirs)))
    packed = (PARTS, LAYERS, 8, 128)
    return mine.reshape(packed), theirs.reshape(packed), fix_lo, fix_hi


def pair_kernel(mine, other, sent, kept):
    first_core = is_first_core()
    for l in range(LAYERS):
        a = [mine[part, l] for part in range(PARTS)]
        b = [other[part, l] for part in range(PARTS)]
        lo = [jnp.where(first_core, x, y) for x, y in zip(a, b)]
        hi = [jnp.where(first_core, y, x) for x, y in zip(a, b)]
        face = jnp.minimum(lo[CDN], hi[CD0])
        down = face + jnp.where(lo[CDN] > 0.0, hi[WA0], 0.0)
        scale = 1.0 / (lo[DN] * (hi[D0] + down) + face * hi[D0])
        in_b = scale * (hi[D0] + down)
        in_g = scale * face
        in_w = scale * down
        in_a = scale * (lo[DN] + face)
        last_f, last_l = in_b * lo[EN], in_g * hi[F0]
        first_f, first_l = in_w * lo[EN], in_a * hi[F0]
        last_r = [in_b * lo[RN + t] + in_g * hi[R0 + t] for t in range(TRACERS)]
        first_r = [in_w * lo[RN + t] + in_a * hi[R0 + t] for t in range(TRACERS)]
        out = [None] * PARTS
        out[CD0], out[WA0], out[CDN] = lo[CD0], lo[WA0], hi[CDN]
        out[D0] = lo[D0] - lo[F0] * last_f
        out[F0] = lo[F0] * last_l
        out[DN] = hi[DN] - hi[EN] * first_l
        out[EN] = hi[EN] * first_f
        for t in range(TRACERS):
            out[R0 + t] = lo[R0 + t] + lo[F0] * last_r[t]
            out[RN + t] = hi[RN + t] + hi[EN] * first_r[t]
        for part in range(PARTS):
            sent[pl.ds(l * SENT + part, CHIPS, stride=LAYERS * SENT), :] = out[part]
        sent[pl.ds(l * SENT + PARTS, CHIPS, stride=LAYERS * SENT), :] = jnp.zeros((8, 128), F32)
        for k, value in enumerate(last_r + first_r + [last_f, last_l, first_f, first_l]):
            kept[k, l] = value


def pair_part(mine, other):
    vmem = pl.BlockSpec(memory_space=pltpu.VMEM)
    return pl.pallas_call(
        pair_kernel,
        in_specs=[vmem, vmem],
        out_specs=[vmem, vmem],
        out_shape=[
            jax.ShapeDtypeStruct((CHIPS * LAYERS * SENT, 128), F32),
            jax.ShapeDtypeStruct((14, LAYERS, 8, 128), F32),
        ],
        compiler_params=SMALL,
        name="pair_part",
    )(mine, other)


def chain_kernel(parts, solved):
    load = lambda chip, part: parts[pl.ds(chip * LAYERS * SENT + part, LAYERS, stride=SENT), :]
    firsts, lasts = [], []
    cd_prev = gate = ratio = reduced = None
    base, known = None, None
    for chip in range(CHIPS):
        d0, f0 = load(chip, D0), load(chip, F0)
        dn, en = load(chip, DN), load(chip, EN)
        r0 = [load(chip, R0 + t) for t in range(TRACERS)]
        rn = [load(chip, RN + t) for t in range(TRACERS)]
        if chip:
            cd0 = load(chip, CD0)
            face = jnp.minimum(cd_prev, cd0)
            down = face + jnp.where(cd_prev > 0.0, load(chip, WA0), 0.0)
            inverse = 1.0 / (base + face)
            ratio = face * inverse
            reduced = [x * inverse for x in known]
            lasts.append((ratio, reduced))
            inverse = 1.0 / (d0 + down * (1.0 - ratio))
            r0 = [x + down * y for x, y in zip(r0, reduced)]
        else:
            inverse = 1.0 / d0
        ahead = f0 * inverse
        here = [x * inverse for x in r0]
        firsts.append((ahead, here))
        base = dn - en * ahead
        known = [x + en * y for x, y in zip(rn, here)]
        cd_prev = load(chip, CDN)
    inverse = 1.0 / base
    last = [x * inverse for x in known]
    for chip in reversed(range(CHIPS)):
        ahead, here = firsts[chip]
        first = [x + ahead * y for x, y in zip(here, last)]
        for t in range(TRACERS):
            solved[pl.ds(chip * LAYERS * BACK + t, LAYERS, stride=BACK), :] = first[t]
            solved[pl.ds(chip * LAYERS * BACK + TRACERS + t, LAYERS, stride=BACK), :] = last[t]
        if chip:
            ratio, reduced = lasts[chip - 1]
            last = [x + ratio * y for x, y in zip(reduced, first)]


def chain_part(parts):
    vmem = pl.BlockSpec(memory_space=pltpu.VMEM)
    return pl.pallas_call(
        chain_kernel,
        in_specs=[vmem],
        out_specs=vmem,
        out_shape=jax.ShapeDtypeStruct((CHIPS * LAYERS * BACK, 128), F32),
        compiler_params=SMALL,
        name="chain_part",
    )(parts)


def middle_kernel(solved, kept, mine, theirs):
    first_core = is_first_core()
    for l in range(LAYERS):
        last_f, last_l, first_f, first_l = (kept[10 + k, l] for k in range(4))
        for t in range(TRACERS):
            first = solved[pl.ds(l * BACK + t, CHIPS, stride=LAYERS * BACK), :]
            last = solved[pl.ds(l * BACK + TRACERS + t, CHIPS, stride=LAYERS * BACK), :]
            before = kept[t, l] + last_f * first + last_l * last
            after = kept[TRACERS + t, l] + first_f * first + first_l * last
            mine[t, l] = jnp.where(first_core, first, after)
            mine[TRACERS + t, l] = jnp.where(first_core, before, last)
            theirs[t, l] = jnp.where(first_core, after, first)
            theirs[TRACERS + t, l] = jnp.where(first_core, last, before)


def middle_part(solved, kept):
    vmem = pl.BlockSpec(memory_space=pltpu.VMEM)
    return pl.pallas_call(
        middle_kernel,
        in_specs=[vmem, vmem],
        out_specs=[vmem, vmem],
        out_shape=[jax.ShapeDtypeStruct((BACK, LAYERS, 8, 128), F32)] * 2,
        compiler_params=SMALL,
        name="middle_part",
    )(solved, kept)


def spread_kernel(red, fill, rho, fix_lo, fix_hi, base, of_first, of_last):
    lane = lax.broadcasted_iota(jnp.int32, (8, 128), 1)
    zero, one = jnp.zeros((8, 128), F32), jnp.ones((8, 128), F32)

    def one_layer(layer, none):
        for half in range(2):
            for row, first, last in ((0, one, zero), (ROWS - 1, zero, one)):
                of_first[layer, line(row, half), :] = first
                of_last[layer, line(row, half), :] = last
                for t in range(TRACERS):
                    base[t, layer, line(row, half), :] = zero
            values, first, last = [zero] * TRACERS, zero, one
            for row in reversed(range(1, ROWS - 1)):
                where = pl.ds((half * ROWS + row) * 8, 8)
                ratio = rho[layer, where, :]
                first = fill[layer, where, :] + ratio * first
                last = ratio * last
                of_first[layer, line(row, half), :] = first
                of_last[layer, line(row, half), :] = last
                for t in range(TRACERS):
                    values[t] = red[t, layer, where, :] + ratio * values[t]
                    base[t, layer, line(row, half), :] = values[t]
        for i in range(2):
            for fix, at, column in ((fix_lo, 0, 0), (fix_hi, 127, 15)):
                change = fix[pl.ds(layer * ROWS + i * 8, 8), :]
                for t in range(TRACERS):
                    where = tile(i, column)
                    moved = jnp.where(lane == at, pltpu.roll(change, (at - t) % 128, 1), 0.0)
                    base[t, layer, where, :] = base[t, layer, where, :] + moved

    lax.fori_loop(0, LAYERS, one_layer, None)


def spread_part(red, fill, rho, fix_lo, fix_hi):
    vmem = pl.BlockSpec(memory_space=pltpu.VMEM)
    layered = jax.ShapeDtypeStruct((LAYERS, 256, 128), F32)
    return pl.pallas_call(
        spread_kernel,
        in_specs=[vmem] * 5,
        out_specs=[vmem] * 3,
        out_shape=[jax.ShapeDtypeStruct((TRACERS, LAYERS, 256, 128), F32), layered, layered],
        compiler_params=pltpu.CompilerParams(vmem_limit_bytes=12 * 1024 * 1024),
        name="spread_part",
    )(red, fill, rho, fix_lo, fix_hi)


def final_kernel(base, of_first, of_last, mine, other, out, ready, sems):
    first_core = is_first_core()

    def copy_of(layer):
        return pltpu.make_async_copy(ready.at[:, layer], out.at[:, layer], sems.at[layer])

    def one_layer(layer, none):
        def fill_in(low, high):
            for half, ends in ((0, low), (1, high)):
                for j in range(8):
                    spread = lambda k: jnp.broadcast_to(ends[k, layer, pl.ds(j, 1), :], (8, 128))
                    firsts = [spread(t) for t in range(TRACERS)]
                    lasts = [spread(TRACERS + t) for t in range(TRACERS)]
                    for i in range(2):
                        where = tile(i, half * 8 + j)
                        by_first, by_last = of_first[layer, where, :], of_last[layer, where, :]
                        for t in range(TRACERS):
                            ready[t, layer, where, :] = (
                                base[t, layer, where, :] + by_first * firsts[t] + by_last * lasts[t]
                            )

        pl.when(first_core)(lambda: fill_in(mine, other))
        pl.when(jnp.logical_not(first_core))(lambda: fill_in(other, mine))
        copy_of(layer).start()

    lax.fori_loop(0, LAYERS, one_layer, None)
    for layer in range(LAYERS):
        copy_of(layer).wait()


def final_part(base, of_first, of_last, mine, other):
    vmem = pl.BlockSpec(memory_space=pltpu.VMEM)
    return pl.pallas_call(
        final_kernel,
        in_specs=[vmem] * 5,
        out_specs=pl.BlockSpec(memory_space=pltpu.HBM),
        out_shape=jax.ShapeDtypeStruct((TRACERS, LAYERS, 256, 128), F32),
        scratch_shapes=[
            pltpu.VMEM((TRACERS, LAYERS, 256, 128), F32),
            pltpu.SemaphoreType.DMA((LAYERS,)),
        ],
        compiler_params=pltpu.CompilerParams(vmem_limit_bytes=12 * 1024 * 1024),
        name="final_part",
    )(base, of_first, of_last, mine, other)


def on_device(tracers, kappa_x, kappa_y, courant, wet_mask, levels):
    count = lax.axis_size("cross")
    pairs = [(i, i ^ 1) for i in range(2 * CHIPS)]
    lines = [[c + 2 * z for z in range(CHIPS)] for c in range(2)]

    lowest, highest = edges(tracers, kappa_y, wet_mask, levels)
    left = lax.ppermute(highest, "cross", [(i, (i + 1) % count) for i in range(count)])
    right = lax.ppermute(lowest, "cross", [((i + 1) % count, i) for i in range(count)])
    red, fill, rho, inv, gain, mine, theirs = local_part(
        folded(tracers),
        folded(kappa_x),
        folded(kappa_y),
        folded(courant),
        folded(wet_mask),
        folded(levels),
    )
    mine, theirs, fix_lo, fix_hi = outer_part(
        lowest, highest, left, right, inv, gain, rho, mine, theirs
    )
    other = lax.ppermute(theirs, "chan", pairs)
    base, of_first, of_last = spread_part(red, fill, rho, fix_lo, fix_hi)
    sent, kept = pair_part(mine, other)
    parts = lax.all_to_all(
        sent.reshape(CHIPS, LAYERS * SENT, 128), "chan", 0, 0, axis_index_groups=lines, tiled=True
    )
    solved = chain_part(parts.reshape(CHIPS * LAYERS * SENT, 128))
    back = lax.all_to_all(
        solved.reshape(CHIPS, LAYERS * BACK, 128), "chan", 0, 0, axis_index_groups=lines, tiled=True
    )
    mine, theirs = middle_part(back.reshape(CHIPS * LAYERS * BACK, 128), kept)
    other = lax.ppermute(theirs, "chan", pairs)
    return unfolded(final_part(base, of_first, of_last, mine, other))


def solution(mesh):
    placed = (
        P(None, None, "chan", "cross"),
        P(None, "chan", "cross"),
        P(None, "chan", "cross"),
        P(None, "chan", "cross"),
        P("chan", "cross"),
        P("chan", "cross"),
    )
    return jax.shard_map(
        on_device,
        mesh=mesh,
        in_specs=placed,
        out_specs=P(None, None, "chan", "cross"),
        check_vma=False,
    )
```

```python
import functools

import jax
import jax.numpy as jnp
from jax import lax
from jax.experimental import pallas as pl
from jax.experimental.pallas import tpu as pltpu
from jax.sharding import PartitionSpec as P

TRACERS = 5
LAYERS = 4
ROWS = 16
CHIPS = 8
CD0, WA0, D0, F0, R0, CDN, DN, EN, RN = 0, 1, 2, 3, 4, 9, 10, 11, 12
PARTS = 17
SENT = 18
BACK = 10
F32 = jnp.float32
SMALL = pltpu.CompilerParams(vmem_limit_bytes=4 * 1024 * 1024)


def folded(cells):
    lead = cells.shape[:-2]
    cells = cells.reshape(lead + (2, 8, 16, 128))
    return jnp.swapaxes(cells, len(lead) + 1, len(lead) + 2).reshape(lead + (256, 128))


def unfolded(cells):
    lead = cells.shape[:-2]
    cells = cells.reshape(lead + (2, 16, 8, 128))
    return jnp.swapaxes(cells, len(lead) + 1, len(lead) + 2).reshape(lead + (16, 2048))


def in_hbm(cells):
    return pltpu.with_memory_space_constraint(cells, pltpu.HBM)


def line(row, half):
    return pl.ds((row // 8) * 128 + half * 64 + row % 8, 8, stride=8)


def is_first_core():
    return lax.axis_index("chan") % 2 == 0


def tile(row_tile, column_tile):
    return pl.ds(row_tile * 128 + column_tile * 8, 8)


def edges_kernel(tr_lo, tr_hi, ky_lo, ky_hi, wet_lo, wet_hi, lev_lo, lev_hi, out_lo, out_hi):
    lane = lax.broadcasted_iota(jnp.int32, (8, 128), 1)
    for tr, ky, wet, lev, out, at in (
        (tr_lo, ky_lo, wet_lo, lev_lo, out_lo, 0),
        (tr_hi, ky_hi, wet_hi, lev_hi, out_hi, 127),
    ):
        for l in range(LAYERS):
            for i in range(2):
                rows = pl.ds(i * 8, 8)
                active = (wet[rows, :] > 0) & (lev[rows, :] > l)
                cross = jnp.where(active, ky[l, rows, :], 0.0)
                packed = jnp.where(lane < 64, 0.0, jnp.broadcast_to(cross[:, at : at + 1], (8, 128)))
                for t in range(TRACERS):
                    packed = jnp.where(lane == t, pltpu.roll(tr[t, l, rows, :], (t - at) % 128, 1), packed)
                out[l, rows, :] = packed


def edges(tracers, kappa_y, wet, levels):
    def spec(lead, at):
        zeros = (0,) * (len(lead) + 1)
        return pl.BlockSpec(lead + (16, 128), lambda i, zeros=zeros, at=at: zeros + (at,))

    return pl.pallas_call(
        edges_kernel,
        grid=(1,),
        in_specs=[
            spec((TRACERS, LAYERS), 0),
            spec((TRACERS, LAYERS), 15),
            spec((LAYERS,), 0),
            spec((LAYERS,), 15),
            spec((), 0),
            spec((), 15),
            spec((), 0),
            spec((), 15),
        ],
        out_specs=[pl.BlockSpec((LAYERS, 16, 128), lambda i: (0, 0, 0))] * 2,
        out_shape=[jax.ShapeDtypeStruct((LAYERS, 16, 128), F32)] * 2,
        compiler_params=SMALL,
        name="edges",
    )(*(in_hbm(x) for x in (tracers, tracers, kappa_y, kappa_y, wet, wet, levels, levels)))


def local_kernel(
    tr, kx_hbm, ky, co_hbm, wet, lev, red, fill, rho, inv, gain, mine, theirs, side, kx, co, shift, moved, sems
):
    copies = [
        pltpu.make_async_copy(kx_hbm, kx, sems.at[0]),
        pltpu.make_async_copy(co_hbm, co, sems.at[1]),
    ]
    for copy in copies:
        copy.start()
    source = lax.broadcasted_iota(jnp.int32, (256, 256), 0) % 128
    target = lax.broadcasted_iota(jnp.int32, (256, 256), 1)
    wanted = jnp.where(target < 128, target + 1, target + 127) % 128
    shift[...] = jnp.where(source == wanted, 1.0, 0.0).astype(jnp.bfloat16)
    lax.fori_loop(
        0, LAYERS, lambda layer, none: right_sides(layer, tr, ky, wet, lev, side, shift, moved), None
    )
    for copy in copies:
        copy.wait()
    eliminate_bands(kx, co, wet, lev, fill, rho, inv, gain, mine, theirs)
    lax.fori_loop(
        0, LAYERS, lambda layer, none: eliminate_sides(layer, red, rho, inv, gain, mine, theirs, side), None
    )


def right_sides(layer, tr, ky, wet, lev, side, shift, moved):
    lane = lax.broadcasted_iota(jnp.int32, (8, 128), 1)
    head, tail = lane == 0, lane == 127

    def move(k, cells):
        coarse = cells.astype(jnp.bfloat16)
        rest = (cells - coarse.astype(F32)).astype(jnp.bfloat16)
        moved[k] = jnp.dot(
            jnp.concatenate([coarse, rest], axis=1), shift[...], preferred_element_type=F32
        )

    def ahead(k, i, j):
        here = moved[k, tile(i, j), 0:128]
        return here if j == 15 else jnp.where(tail, moved[k, tile(i, j + 1), 0:128], here)

    def behind(k, i, j):
        here = moved[k, tile(i, j), 128:256]
        return here if j == 0 else jnp.where(head, moved[k, tile(i, j - 1), 128:256], here)

    cross = jnp.where((wet[...] > 0) & (lev[...] > layer), ky[layer], 0.0)
    move(TRACERS, cross)
    for t in range(TRACERS):
        move(t, tr[t, layer])
    for i in range(2):
        for j in range(16):
            now = cross[i * 128 + j * 8 : i * 128 + j * 8 + 8]
            upper = jnp.minimum(now, ahead(TRACERS, i, j))
            lower = jnp.minimum(now, behind(TRACERS, i, j))
            if j == 15:
                upper = jnp.where(tail, 0.0, upper)
            if j == 0:
                lower = jnp.where(head, 0.0, lower)
            for t in range(TRACERS):
                centre = tr[t, layer, tile(i, j), :]
                side[layer, t, tile(i, j), :] = (
                    centre + upper * (ahead(t, i, j) - centre) - lower * (centre - behind(t, i, j))
                )


def row_of(half, row):
    return pl.ds((half * ROWS + row) * 8, 8)


def put(mine, theirs, part, layer, halves):
    first_core = is_first_core()
    mine[part, layer] = jnp.where(first_core, halves[0], halves[1])
    theirs[part, layer] = jnp.where(first_core, halves[1], halves[0])


def eliminate_bands(kx, co, wet, lev, fill, rho, inv, gain, mine, theirs):
    groups = [(layer, half) for layer in range(LAYERS) for half in range(2)]
    depth = [lev[line(0, half), :] for half in range(2)]
    deep = {g: depth[g[1]] > g[0] for g in groups}

    def load(row):
        diff, flow = {}, {}
        for half in range(2):
            where = line(row, half)
            water = wet[where, :] > 0
            for layer in range(LAYERS):
                g = layer, half
                active = water & deep[g]
                diff[g] = jnp.where(active, kx[layer, where, :], 0.0)
                flow[g] = jnp.where(active, co[layer, where, :], 0.0)
        return diff, flow

    def put_all(part, values):
        for layer in range(LAYERS):
            put(mine, theirs, part, layer, [values[layer, half] for half in range(2)])

    before, flow = load(0)
    put_all(CD0, before)
    put_all(WA0, flow)
    now, flow = load(1)
    first = {g: jnp.minimum(before[g], now[g]) for g in groups}
    for layer, half in groups:
        gain[layer, row_of(half, 0), :] = first[layer, half]
    down = dict(first)
    ratio, fills, sums, chain = {}, {}, {}, {}
    for row in range(1, ROWS - 1):
        after, flow_after = load(row + 1)
        for g in groups:
            layer, half = g
            where = row_of(half, row)
            up = jnp.minimum(now[g], after[g])
            low = down[g] + jnp.where(before[g] > 0.0, flow[g], 0.0)
            if row == 1:
                inverse = 1.0 / (1.0 + up + low)
                ratio[g] = up * inverse
                gained = low * inverse
                fills[g] = gained
                sums[g] = gained
                chain[g] = ratio[g]
            else:
                inverse = 1.0 / (1.0 + up + low * (1.0 - ratio[g]))
                ratio[g] = up * inverse
                gained = low * inverse
                fills[g] = gained * fills[g]
                sums[g] = sums[g] + chain[g] * fills[g]
                chain[g] = chain[g] * ratio[g]
            inv[layer, where, :] = inverse
            gain[layer, where, :] = gained
            rho[layer, where, :] = ratio[g]
            fill[layer, where, :] = fills[g]
            down[g] = up
        before, now, flow = now, after, flow_after
    low = {g: down[g] + jnp.where(before[g] > 0.0, flow[g], 0.0) for g in groups}
    for layer, half in groups:
        gain[layer, row_of(half, ROWS - 1), :] = low[layer, half]
    put_all(CDN, now)
    put_all(D0, {g: 1.0 + first[g] * (1.0 - sums[g]) for g in groups})
    put_all(F0, {g: first[g] * chain[g] for g in groups})
    put_all(DN, {g: 1.0 + low[g] * (1.0 - ratio[g]) for g in groups})
    put_all(EN, {g: low[g] * fills[g] for g in groups})


def eliminate_sides(layer, red, rho, inv, gain, mine, theirs, side):
    edges_of = []
    for half in range(2):
        get = lambda t, row: side[layer, t, line(row, half), :]
        for row in range(1, ROWS - 1):
            where = row_of(half, row)
            inverse, ratio = inv[layer, where, :], rho[layer, where, :]
            if row == 1:
                reds = [get(t, row) * inverse for t in range(TRACERS)]
                sums = list(reds)
                chain = ratio
            else:
                gained = gain[layer, where, :]
                reds = [get(t, row) * inverse + gained * reds[t] for t in range(TRACERS)]
                sums = [sums[t] + chain * reds[t] for t in range(TRACERS)]
                chain = chain * ratio
            for t in range(TRACERS):
                red[t, layer, where, :] = reds[t]
        first, low = gain[layer, row_of(half, 0), :], gain[layer, row_of(half, ROWS - 1), :]
        edges_of.append(
            [get(t, 0) + first * sums[t] for t in range(TRACERS)]
            + [get(t, ROWS - 1) + low * reds[t] for t in range(TRACERS)]
        )
    for t in range(TRACERS):
        for part, k in ((R0 + t, t), (RN + t, TRACERS + t)):
            put(mine, theirs, part, layer, [edges_of[0][k], edges_of[1][k]])


def local_part(tracers, kappa_x, kappa_y, courant, wet, levels):
    vmem = pl.BlockSpec(memory_space=pltpu.VMEM)
    hbm = pl.BlockSpec(memory_space=pltpu.HBM)
    layered = jax.ShapeDtypeStruct((LAYERS, 256, 128), F32)
    packed = jax.ShapeDtypeStruct((PARTS, LAYERS, 8, 128), F32)
    return pl.pallas_call(
        local_kernel,
        in_specs=[vmem, hbm, vmem, hbm, vmem, vmem],
        out_specs=[vmem] * 7,
        out_shape=[jax.ShapeDtypeStruct((TRACERS, LAYERS, 256, 128), F32)] + [layered] * 4 + [packed] * 2,
        scratch_shapes=[
            pltpu.VMEM((LAYERS, TRACERS, 256, 128), F32),
            pltpu.VMEM((LAYERS, 256, 128), F32),
            pltpu.VMEM((LAYERS, 256, 128), F32),
            pltpu.VMEM((256, 256), jnp.bfloat16),
            pltpu.VMEM((TRACERS + 1, 256, 256), F32),
            pltpu.SemaphoreType.DMA((2,)),
        ],
        compiler_params=pltpu.CompilerParams(vmem_limit_bytes=12 * 1024 * 1024),
        name="local_part",
    )(tracers, in_hbm(kappa_x), kappa_y, in_hbm(courant), wet, levels)


def outer_kernel(
    own_lo, own_hi, left, right, inv, gain, rho, mine_in, theirs_in, mine, theirs, fix_lo, fix_hi
):
    place = lax.axis_index("cross")
    first_core = is_first_core()
    mine[...] = mine_in[...]
    theirs[...] = theirs_in[...]
    lane = lax.broadcasted_iota(jnp.int32, (LAYERS, 128), 1)
    for e, (own, halo, fix) in enumerate(((own_lo, left, fix_lo), (own_hi, right, fix_hi))):
        at, sub = (0, 0) if e == 0 else (127, 7)
        inside = (place > 0) if e == 0 else (place < lax.axis_size("cross") - 1)

        def coefficient(ref, row):
            values = ref[pl.ds((e * ROWS + row) * 8 + sub, LAYERS, stride=256), :]
            return jnp.broadcast_to(values[:, at : at + 1], (LAYERS, 128))

        deltas = []
        for row in range(ROWS):
            here = own[pl.ds(row, LAYERS, stride=ROWS), :]
            there = jnp.where(inside, halo[pl.ds(row, LAYERS, stride=ROWS), :], 0.0)
            face = pltpu.roll(jnp.minimum(here, there), 64, 1)
            deltas.append(face * (there - here))
        rhos = [None] + [coefficient(rho, row) for row in range(1, ROWS - 1)]
        reds = [None] * ROWS
        for row in range(1, ROWS - 1):
            reds[row] = deltas[row] * coefficient(inv, row)
            if row == 1:
                total, chain = reds[1], rhos[1]
            else:
                reds[row] = reds[row] + coefficient(gain, row) * reds[row - 1]
                total = total + chain * reds[row]
                chain = chain * rhos[row]
        first = deltas[0] + coefficient(gain, 0) * total
        last = deltas[ROWS - 1] + coefficient(gain, ROWS - 1) * reds[ROWS - 2]
        zero = jnp.zeros((LAYERS, 128), F32)
        fix[pl.ds(0, LAYERS, stride=ROWS), :] = zero
        fix[pl.ds(ROWS - 1, LAYERS, stride=ROWS), :] = zero
        value = zero
        for row in reversed(range(1, ROWS - 1)):
            value = reds[row] + rhos[row] * value
            fix[pl.ds(row, LAYERS, stride=ROWS), :] = value

        def add_to(ref):
            for t in range(TRACERS):
                for part, change in ((R0 + t, first), (RN + t, last)):
                    rows = pl.ds(part * LAYERS * 8 + sub, LAYERS, stride=8)
                    ref[rows, :] = ref[rows, :] + jnp.where(lane == at, pltpu.roll(change, (at - t) % 128, 1), 0.0)

        pl.when(first_core if e == 0 else jnp.logical_not(first_core))(lambda: add_to(mine))
        pl.when(jnp.logical_not(first_core) if e == 0 else first_core)(lambda: add_to(theirs))


def outer_part(own_lo, own_hi, left, right, inv, gain, rho, mine, theirs):
    vmem = pl.BlockSpec(memory_space=pltpu.VMEM)
    flat = lambda x: x.reshape(-1, 128)
    mine, theirs, fix_lo, fix_hi = pl.pallas_call(
        outer_kernel,
        in_specs=[vmem] * 9,
        out_specs=[vmem] * 4,
        out_shape=[jax.ShapeDtypeStruct((PARTS * LAYERS * 8, 128), F32)] * 2
        + [jax.ShapeDtypeStruct((LAYERS * ROWS, 128), F32)] * 2,
        compiler_params=SMALL,
        name="outer_part",
    )(*(flat(x) for x in (own_lo, own_hi, left, right, inv, gain, rho, mine, theirs)))
    packed = (PARTS, LAYERS, 8, 128)
    return mine.reshape(packed), theirs.reshape(packed), fix_lo, fix_hi


def pair_kernel(mine, other, sent, kept):
    first_core = is_first_core()
    for l in range(LAYERS):
        a = [mine[part, l] for part in range(PARTS)]
        b = [other[part, l] for part in range(PARTS)]
        lo = [jnp.where(first_core, x, y) for x, y in zip(a, b)]
        hi = [jnp.where(first_core, y, x) for x, y in zip(a, b)]
        face = jnp.minimum(lo[CDN], hi[CD0])
        down = face + jnp.where(lo[CDN] > 0.0, hi[WA0], 0.0)
        scale = 1.0 / (lo[DN] * (hi[D0] + down) + face * hi[D0])
        in_b = scale * (hi[D0] + down)
        in_g = scale * face
        in_w = scale * down
        in_a = scale * (lo[DN] + face)
        last_f, last_l = in_b * lo[EN], in_g * hi[F0]
        first_f, first_l = in_w * lo[EN], in_a * hi[F0]
        last_r = [in_b * lo[RN + t] + in_g * hi[R0 + t] for t in range(TRACERS)]
        first_r = [in_w * lo[RN + t] + in_a * hi[R0 + t] for t in range(TRACERS)]
        out = [None] * PARTS
        out[CD0], out[WA0], out[CDN] = lo[CD0], lo[WA0], hi[CDN]
        out[D0] = lo[D0] - lo[F0] * last_f
        out[F0] = lo[F0] * last_l
        out[DN] = hi[DN] - hi[EN] * first_l
        out[EN] = hi[EN] * first_f
        for t in range(TRACERS):
            out[R0 + t] = lo[R0 + t] + lo[F0] * last_r[t]
            out[RN + t] = hi[RN + t] + hi[EN] * first_r[t]
        for part in range(PARTS):
            sent[pl.ds(l * SENT + part, CHIPS, stride=LAYERS * SENT), :] = out[part]
        sent[pl.ds(l * SENT + PARTS, CHIPS, stride=LAYERS * SENT), :] = jnp.zeros((8, 128), F32)
        for k, value in enumerate(last_r + first_r + [last_f, last_l, first_f, first_l]):
            kept[k, l] = value


def pair_part(mine, other):
    vmem = pl.BlockSpec(memory_space=pltpu.VMEM)
    return pl.pallas_call(
        pair_kernel,
        in_specs=[vmem, vmem],
        out_specs=[vmem, vmem],
        out_shape=[
            jax.ShapeDtypeStruct((CHIPS * LAYERS * SENT, 128), F32),
            jax.ShapeDtypeStruct((14, LAYERS, 8, 128), F32),
        ],
        compiler_params=SMALL,
        name="pair_part",
    )(mine, other)


def chain_kernel(parts, solved):
    load = lambda chip, part: parts[pl.ds(chip * LAYERS * SENT + part, LAYERS, stride=SENT), :]
    firsts, lasts = [], []
    cd_prev = gate = ratio = reduced = None
    base, known = None, None
    for chip in range(CHIPS):
        d0, f0 = load(chip, D0), load(chip, F0)
        dn, en = load(chip, DN), load(chip, EN)
        r0 = [load(chip, R0 + t) for t in range(TRACERS)]
        rn = [load(chip, RN + t) for t in range(TRACERS)]
        if chip:
            cd0 = load(chip, CD0)
            face = jnp.minimum(cd_prev, cd0)
            down = face + jnp.where(cd_prev > 0.0, load(chip, WA0), 0.0)
            inverse = 1.0 / (base + face)
            ratio = face * inverse
            reduced = [x * inverse for x in known]
            lasts.append((ratio, reduced))
            inverse = 1.0 / (d0 + down * (1.0 - ratio))
            r0 = [x + down * y for x, y in zip(r0, reduced)]
        else:
            inverse = 1.0 / d0
        ahead = f0 * inverse
        here = [x * inverse for x in r0]
        firsts.append((ahead, here))
        base = dn - en * ahead
        known = [x + en * y for x, y in zip(rn, here)]
        cd_prev = load(chip, CDN)
    inverse = 1.0 / base
    last = [x * inverse for x in known]
    for chip in reversed(range(CHIPS)):
        ahead, here = firsts[chip]
        first = [x + ahead * y for x, y in zip(here, last)]
        for t in range(TRACERS):
            solved[pl.ds(chip * LAYERS * BACK + t, LAYERS, stride=BACK), :] = first[t]
            solved[pl.ds(chip * LAYERS * BACK + TRACERS + t, LAYERS, stride=BACK), :] = last[t]
        if chip:
            ratio, reduced = lasts[chip - 1]
            last = [x + ratio * y for x, y in zip(reduced, first)]


def chain_part(parts):
    vmem = pl.BlockSpec(memory_space=pltpu.VMEM)
    return pl.pallas_call(
        chain_kernel,
        in_specs=[vmem],
        out_specs=vmem,
        out_shape=jax.ShapeDtypeStruct((CHIPS * LAYERS * BACK, 128), F32),
        compiler_params=SMALL,
        name="chain_part",
    )(parts)


def middle_kernel(solved, kept, mine, theirs):
    first_core = is_first_core()
    for l in range(LAYERS):
        last_f, last_l, first_f, first_l = (kept[10 + k, l] for k in range(4))
        for t in range(TRACERS):
            first = solved[pl.ds(l * BACK + t, CHIPS, stride=LAYERS * BACK), :]
            last = solved[pl.ds(l * BACK + TRACERS + t, CHIPS, stride=LAYERS * BACK), :]
            before = kept[t, l] + last_f * first + last_l * last
            after = kept[TRACERS + t, l] + first_f * first + first_l * last
            mine[t, l] = jnp.where(first_core, first, after)
            mine[TRACERS + t, l] = jnp.where(first_core, before, last)
            theirs[t, l] = jnp.where(first_core, after, first)
            theirs[TRACERS + t, l] = jnp.where(first_core, last, before)


def middle_part(solved, kept):
    vmem = pl.BlockSpec(memory_space=pltpu.VMEM)
    return pl.pallas_call(
        middle_kernel,
        in_specs=[vmem, vmem],
        out_specs=[vmem, vmem],
        out_shape=[jax.ShapeDtypeStruct((BACK, LAYERS, 8, 128), F32)] * 2,
        compiler_params=SMALL,
        name="middle_part",
    )(solved, kept)


def spread_kernel(red, fill, rho, fix_lo, fix_hi, base, of_first, of_last):
    lane = lax.broadcasted_iota(jnp.int32, (8, 128), 1)
    zero, one = jnp.zeros((8, 128), F32), jnp.ones((8, 128), F32)

    def one_layer(layer, none):
        for half in range(2):
            for row, first, last in ((0, one, zero), (ROWS - 1, zero, one)):
                of_first[layer, line(row, half), :] = first
                of_last[layer, line(row, half), :] = last
                for t in range(TRACERS):
                    base[t, layer, line(row, half), :] = zero
            values, first, last = [zero] * TRACERS, zero, one
            for row in reversed(range(1, ROWS - 1)):
                where = pl.ds((half * ROWS + row) * 8, 8)
                ratio = rho[layer, where, :]
                first = fill[layer, where, :] + ratio * first
                last = ratio * last
                of_first[layer, line(row, half), :] = first
                of_last[layer, line(row, half), :] = last
                for t in range(TRACERS):
                    values[t] = red[t, layer, where, :] + ratio * values[t]
                    base[t, layer, line(row, half), :] = values[t]
        for i in range(2):
            for fix, at, column in ((fix_lo, 0, 0), (fix_hi, 127, 15)):
                change = fix[pl.ds(layer * ROWS + i * 8, 8), :]
                for t in range(TRACERS):
                    where = tile(i, column)
                    moved = jnp.where(lane == at, pltpu.roll(change, (at - t) % 128, 1), 0.0)
                    base[t, layer, where, :] = base[t, layer, where, :] + moved

    lax.fori_loop(0, LAYERS, one_layer, None)


def spread_part(red, fill, rho, fix_lo, fix_hi):
    vmem = pl.BlockSpec(memory_space=pltpu.VMEM)
    layered = jax.ShapeDtypeStruct((LAYERS, 256, 128), F32)
    return pl.pallas_call(
        spread_kernel,
        in_specs=[vmem] * 5,
        out_specs=[vmem] * 3,
        out_shape=[jax.ShapeDtypeStruct((TRACERS, LAYERS, 256, 128), F32), layered, layered],
        compiler_params=pltpu.CompilerParams(vmem_limit_bytes=12 * 1024 * 1024),
        name="spread_part",
    )(red, fill, rho, fix_lo, fix_hi)


def final_kernel(base, of_first, of_last, mine, other, out, ready, sems):
    first_core = is_first_core()

    def copy_of(layer):
        return pltpu.make_async_copy(ready.at[:, layer], out.at[:, layer], sems.at[layer])

    def one_layer(layer, none):
        def fill_in(low, high):
            for half, ends in ((0, low), (1, high)):
                for j in range(8):
                    spread = lambda k: jnp.broadcast_to(ends[k, layer, pl.ds(j, 1), :], (8, 128))
                    firsts = [spread(t) for t in range(TRACERS)]
                    lasts = [spread(TRACERS + t) for t in range(TRACERS)]
                    for i in range(2):
                        where = tile(i, half * 8 + j)
                        by_first, by_last = of_first[layer, where, :], of_last[layer, where, :]
                        for t in range(TRACERS):
                            ready[t, layer, where, :] = (
                                base[t, layer, where, :] + by_first * firsts[t] + by_last * lasts[t]
                            )

        pl.when(first_core)(lambda: fill_in(mine, other))
        pl.when(jnp.logical_not(first_core))(lambda: fill_in(other, mine))
        copy_of(layer).start()

    lax.fori_loop(0, LAYERS, one_layer, None)
    for layer in range(LAYERS):
        copy_of(layer).wait()


def final_part(base, of_first, of_last, mine, other):
    vmem = pl.BlockSpec(memory_space=pltpu.VMEM)
    return pl.pallas_call(
        final_kernel,
        in_specs=[vmem] * 5,
        out_specs=pl.BlockSpec(memory_space=pltpu.HBM),
        out_shape=jax.ShapeDtypeStruct((TRACERS, LAYERS, 256, 128), F32),
        scratch_shapes=[
            pltpu.VMEM((TRACERS, LAYERS, 256, 128), F32),
            pltpu.SemaphoreType.DMA((LAYERS,)),
        ],
        compiler_params=pltpu.CompilerParams(vmem_limit_bytes=12 * 1024 * 1024),
        name="final_part",
    )(base, of_first, of_last, mine, other)


def on_device(tracers, kappa_x, kappa_y, courant, wet_mask, levels):
    count = lax.axis_size("cross")
    pairs = [(i, i ^ 1) for i in range(2 * CHIPS)]
    lines = [[c + 2 * z for z in range(CHIPS)] for c in range(2)]

    lowest, highest = edges(tracers, kappa_y, wet_mask, levels)
    left = lax.ppermute(highest, "cross", [(i, (i + 1) % count) for i in range(count)])
    right = lax.ppermute(lowest, "cross", [((i + 1) % count, i) for i in range(count)])
    red, fill, rho, inv, gain, mine, theirs = local_part(
        folded(tracers),
        folded(kappa_x),
        folded(kappa_y),
        folded(courant),
        folded(wet_mask),
        folded(levels),
    )
    mine, theirs, fix_lo, fix_hi = outer_part(
        lowest, highest, left, right, inv, gain, rho, mine, theirs
    )
    other = lax.ppermute(theirs, "chan", pairs)
    base, of_first, of_last = spread_part(red, fill, rho, fix_lo, fix_hi)
    sent, kept = pair_part(mine, other)
    parts = lax.all_to_all(
        sent.reshape(CHIPS, LAYERS * SENT, 128), "chan", 0, 0, axis_index_groups=lines, tiled=True
    )
    solved = chain_part(parts.reshape(CHIPS * LAYERS * SENT, 128))
    back = lax.all_to_all(
        solved.reshape(CHIPS, LAYERS * BACK, 128), "chan", 0, 0, axis_index_groups=lines, tiled=True
    )
    mine, theirs = middle_part(back.reshape(CHIPS * LAYERS * BACK, 128), kept)
    other = lax.ppermute(theirs, "chan", pairs)
    return unfolded(final_part(base, of_first, of_last, mine, other))


def solution(mesh):
    placed = (
        P(None, None, "chan", "cross"),
        P(None, "chan", "cross"),
        P(None, "chan", "cross"),
        P(None, "chan", "cross"),
        P("chan", "cross"),
        P("chan", "cross"),
    )
    return jax.shard_map(
        on_device,
        mesh=mesh,
        in_specs=placed,
        out_specs=P(None, None, "chan", "cross"),
        check_vma=False,
    )
```

```python
import functools

import jax
import jax.numpy as jnp
from jax import lax
from jax.experimental import pallas as pl
from jax.experimental.pallas import tpu as pltpu
from jax.sharding import PartitionSpec as P

TRACERS = 5
LAYERS = 4
ROWS = 16
CHIPS = 8
CD0, WA0, D0, F0, R0, CDN, DN, EN, RN = 0, 1, 2, 3, 4, 9, 10, 11, 12
PARTS = 17
SENT = 18
BACK = 10
F32 = jnp.float32
SMALL = pltpu.CompilerParams(vmem_limit_bytes=4 * 1024 * 1024)


def folded(cells):
    lead = cells.shape[:-2]
    cells = cells.reshape(lead + (2, 8, 16, 128))
    return jnp.swapaxes(cells, len(lead) + 1, len(lead) + 2).reshape(lead + (256, 128))


def unfolded(cells):
    lead = cells.shape[:-2]
    cells = cells.reshape(lead + (2, 16, 8, 128))
    return jnp.swapaxes(cells, len(lead) + 1, len(lead) + 2).reshape(lead + (16, 2048))


def in_hbm(cells):
    return pltpu.with_memory_space_constraint(cells, pltpu.HBM)


def line(row, half):
    return pl.ds((row // 8) * 128 + half * 64 + row % 8, 8, stride=8)


def is_first_core():
    return lax.axis_index("chan") % 2 == 0


def tile(row_tile, column_tile):
    return pl.ds(row_tile * 128 + column_tile * 8, 8)


def edges_kernel(tr_lo, tr_hi, ky_lo, ky_hi, wet_lo, wet_hi, lev_lo, lev_hi, out_lo, out_hi, swap_a, swap_b):
    even = lax.axis_index("cross") % 2 == 0
    lane = lax.broadcasted_iota(jnp.int32, (8, 128), 1)
    for tr, ky, wet, lev, out, at in (
        (tr_lo, ky_lo, wet_lo, lev_lo, out_lo, 0),
        (tr_hi, ky_hi, wet_hi, lev_hi, out_hi, 127),
    ):
        for l in range(LAYERS):
            for i in range(2):
                rows = pl.ds(i * 8, 8)
                active = (wet[rows, :] > 0) & (lev[rows, :] > l)
                cross = jnp.where(active, ky[l, rows, :], 0.0)
                packed = jnp.where(lane < 64, 0.0, jnp.broadcast_to(cross[:, at : at + 1], (8, 128)))
                for t in range(TRACERS):
                    packed = jnp.where(lane == t, pltpu.roll(tr[t, l, rows, :], (t - at) % 128, 1), packed)
                out[l, rows, :] = packed
    for l in range(LAYERS):
        for i in range(2):
            rows = pl.ds(i * 8, 8)
            lo, hi = out_lo[l, rows, :], out_hi[l, rows, :]
            swap_a[l, rows, :] = jnp.where(even, hi, lo)
            swap_b[l, rows, :] = jnp.where(even, lo, hi)


def edges(tracers, kappa_y, wet, levels):
    def spec(lead, at):
        zeros = (0,) * (len(lead) + 1)
        return pl.BlockSpec(lead + (16, 128), lambda i, zeros=zeros, at=at: zeros + (at,))

    return pl.pallas_call(
        edges_kernel,
        grid=(1,),
        in_specs=[
            spec((TRACERS, LAYERS), 0),
            spec((TRACERS, LAYERS), 15),
            spec((LAYERS,), 0),
            spec((LAYERS,), 15),
            spec((), 0),
            spec((), 15),
            spec((), 0),
            spec((), 15),
        ],
        out_specs=[pl.BlockSpec((LAYERS, 16, 128), lambda i: (0, 0, 0))] * 4,
        out_shape=[jax.ShapeDtypeStruct((LAYERS, 16, 128), F32)] * 4,
        compiler_params=SMALL,
        name="edges",
    )(*(in_hbm(x) for x in (tracers, tracers, kappa_y, kappa_y, wet, wet, levels, levels)))


def local_kernel(
    tr, kx_hbm, ky, co_hbm, wet, lev, red, fill, rho, inv, gain, mine, theirs, side, kx, co, shift, moved, sems
):
    copies = [
        pltpu.make_async_copy(kx_hbm, kx, sems.at[0]),
        pltpu.make_async_copy(co_hbm, co, sems.at[1]),
    ]
    for copy in copies:
        copy.start()
    source = lax.broadcasted_iota(jnp.int32, (256, 256), 0) % 128
    target = lax.broadcasted_iota(jnp.int32, (256, 256), 1)
    wanted = jnp.where(target < 128, target + 1, target + 127) % 128
    shift[...] = jnp.where(source == wanted, 1.0, 0.0).astype(jnp.bfloat16)
    lax.fori_loop(
        0, LAYERS, lambda layer, none: right_sides(layer, tr, ky, wet, lev, side, shift, moved), None
    )
    for copy in copies:
        copy.wait()
    eliminate_bands(kx, co, wet, lev, fill, rho, inv, gain, mine, theirs)
    lax.fori_loop(
        0, LAYERS, lambda layer, none: eliminate_sides(layer, red, rho, inv, gain, mine, theirs, side), None
    )


def right_sides(layer, tr, ky, wet, lev, side, shift, moved):
    lane = lax.broadcasted_iota(jnp.int32, (8, 128), 1)
    head, tail = lane == 0, lane == 127

    def move(k, cells):
        coarse = cells.astype(jnp.bfloat16)
        rest = (cells - coarse.astype(F32)).astype(jnp.bfloat16)
        moved[k] = jnp.dot(
            jnp.concatenate([coarse, rest], axis=1), shift[...], preferred_element_type=F32
        )

    def ahead(k, i, j):
        here = moved[k, tile(i, j), 0:128]
        return here if j == 15 else jnp.where(tail, moved[k, tile(i, j + 1), 0:128], here)

    def behind(k, i, j):
        here = moved[k, tile(i, j), 128:256]
        return here if j == 0 else jnp.where(head, moved[k, tile(i, j - 1), 128:256], here)

    cross = jnp.where((wet[...] > 0) & (lev[...] > layer), ky[layer], 0.0)
    move(TRACERS, cross)
    for t in range(TRACERS):
        move(t, tr[t, layer])
    for i in range(2):
        for j in range(16):
            now = cross[i * 128 + j * 8 : i * 128 + j * 8 + 8]
            upper = jnp.minimum(now, ahead(TRACERS, i, j))
            lower = jnp.minimum(now, behind(TRACERS, i, j))
            if j == 15:
                upper = jnp.where(tail, 0.0, upper)
            if j == 0:
                lower = jnp.where(head, 0.0, lower)
            for t in range(TRACERS):
                centre = tr[t, layer, tile(i, j), :]
                side[layer, t, tile(i, j), :] = (
                    centre + upper * (ahead(t, i, j) - centre) - lower * (centre - behind(t, i, j))
                )


def row_of(half, row):
    return pl.ds((half * ROWS + row) * 8, 8)


def put(mine, theirs, part, layer, halves):
    first_core = is_first_core()
    mine[part, layer] = jnp.where(first_core, halves[0], halves[1])
    theirs[part, layer] = jnp.where(first_core, halves[1], halves[0])


def eliminate_bands(kx, co, wet, lev, fill, rho, inv, gain, mine, theirs):
    groups = [(layer, half) for layer in range(LAYERS) for half in range(2)]
    depth = [lev[line(0, half), :] for half in range(2)]
    deep = {g: depth[g[1]] > g[0] for g in groups}

    def load(row):
        diff, flow = {}, {}
        for half in range(2):
            where = line(row, half)
            water = wet[where, :] > 0
            for layer in range(LAYERS):
                g = layer, half
                active = water & deep[g]
                diff[g] = jnp.where(active, kx[layer, where, :], 0.0)
                flow[g] = jnp.where(active, co[layer, where, :], 0.0)
        return diff, flow

    def put_all(part, values):
        for layer in range(LAYERS):
            put(mine, theirs, part, layer, [values[layer, half] for half in range(2)])

    before, flow = load(0)
    put_all(CD0, before)
    put_all(WA0, flow)
    now, flow = load(1)
    first = {g: jnp.minimum(before[g], now[g]) for g in groups}
    for layer, half in groups:
        gain[layer, row_of(half, 0), :] = first[layer, half]
    down = dict(first)
    ratio, fills, sums, chain = {}, {}, {}, {}
    for row in range(1, ROWS - 1):
        after, flow_after = load(row + 1)
        for g in groups:
            layer, half = g
            where = row_of(half, row)
            up = jnp.minimum(now[g], after[g])
            low = down[g] + jnp.where(before[g] > 0.0, flow[g], 0.0)
            if row == 1:
                inverse = 1.0 / (1.0 + up + low)
                ratio[g] = up * inverse
                gained = low * inverse
                fills[g] = gained
                sums[g] = gained
                chain[g] = ratio[g]
            else:
                inverse = 1.0 / (1.0 + up + low * (1.0 - ratio[g]))
                ratio[g] = up * inverse
                gained = low * inverse
                fills[g] = gained * fills[g]
                sums[g] = sums[g] + chain[g] * fills[g]
                chain[g] = chain[g] * ratio[g]
            inv[layer, where, :] = inverse
            gain[layer, where, :] = gained
            rho[layer, where, :] = ratio[g]
            fill[layer, where, :] = fills[g]
            down[g] = up
        before, now, flow = now, after, flow_after
    low = {g: down[g] + jnp.where(before[g] > 0.0, flow[g], 0.0) for g in groups}
    for layer, half in groups:
        gain[layer, row_of(half, ROWS - 1), :] = low[layer, half]
    put_all(CDN, now)
    put_all(D0, {g: 1.0 + first[g] * (1.0 - sums[g]) for g in groups})
    put_all(F0, {g: first[g] * chain[g] for g in groups})
    put_all(DN, {g: 1.0 + low[g] * (1.0 - ratio[g]) for g in groups})
    put_all(EN, {g: low[g] * fills[g] for g in groups})


def eliminate_sides(layer, red, rho, inv, gain, mine, theirs, side):
    edges_of = []
    for half in range(2):
        get = lambda t, row: side[layer, t, line(row, half), :]
        for row in range(1, ROWS - 1):
            where = row_of(half, row)
            inverse, ratio = inv[layer, where, :], rho[layer, where, :]
            if row == 1:
                reds = [get(t, row) * inverse for t in range(TRACERS)]
                sums = list(reds)
                chain = ratio
            else:
                gained = gain[layer, where, :]
                reds = [get(t, row) * inverse + gained * reds[t] for t in range(TRACERS)]
                sums = [sums[t] + chain * reds[t] for t in range(TRACERS)]
                chain = chain * ratio
            for t in range(TRACERS):
                red[t, layer, where, :] = reds[t]
        first, low = gain[layer, row_of(half, 0), :], gain[layer, row_of(half, ROWS - 1), :]
        edges_of.append(
            [get(t, 0) + first * sums[t] for t in range(TRACERS)]
            + [get(t, ROWS - 1) + low * reds[t] for t in range(TRACERS)]
        )
    for t in range(TRACERS):
        for part, k in ((R0 + t, t), (RN + t, TRACERS + t)):
            put(mine, theirs, part, layer, [edges_of[0][k], edges_of[1][k]])


def local_part(tracers, kappa_x, kappa_y, courant, wet, levels):
    vmem = pl.BlockSpec(memory_space=pltpu.VMEM)
    hbm = pl.BlockSpec(memory_space=pltpu.HBM)
    layered = jax.ShapeDtypeStruct((LAYERS, 256, 128), F32)
    packed = jax.ShapeDtypeStruct((PARTS, LAYERS, 8, 128), F32)
    return pl.pallas_call(
        local_kernel,
        in_specs=[vmem, hbm, vmem, hbm, vmem, vmem],
        out_specs=[vmem] * 7,
        out_shape=[jax.ShapeDtypeStruct((TRACERS, LAYERS, 256, 128), F32)] + [layered] * 4 + [packed] * 2,
        scratch_shapes=[
            pltpu.VMEM((LAYERS, TRACERS, 256, 128), F32),
            pltpu.VMEM((LAYERS, 256, 128), F32),
            pltpu.VMEM((LAYERS, 256, 128), F32),
            pltpu.VMEM((256, 256), jnp.bfloat16),
            pltpu.VMEM((TRACERS + 1, 256, 256), F32),
            pltpu.SemaphoreType.DMA((2,)),
        ],
        compiler_params=pltpu.CompilerParams(vmem_limit_bytes=12 * 1024 * 1024),
        name="local_part",
    )(tracers, in_hbm(kappa_x), kappa_y, in_hbm(courant), wet, levels)


def inner_kernel(cells, out):
    place = lax.axis_index("cross")
    inner = (place > 0) & (place < lax.axis_size("cross") - 1)
    out[...] = jnp.where(inner, cells[...], 0.0)


def inner_part(cells):
    vmem = pl.BlockSpec(memory_space=pltpu.VMEM)
    return pl.pallas_call(
        inner_kernel,
        in_specs=[vmem],
        out_specs=vmem,
        out_shape=jax.ShapeDtypeStruct(cells.shape, F32),
        compiler_params=SMALL,
        name="inner_part",
    )(cells)


def outer_kernel(
    own_lo, own_hi, from_a, from_b, inv, gain, rho, mine_in, theirs_in, mine, theirs, fix_lo, fix_hi
):
    even = lax.axis_index("cross") % 2 == 0
    first_core = is_first_core()
    mine[...] = mine_in[...]
    theirs[...] = theirs_in[...]
    lane = lax.broadcasted_iota(jnp.int32, (LAYERS, 128), 1)
    for e, (own, (of_even, of_odd), fix) in enumerate(((own_lo, (from_b, from_a), fix_lo), (own_hi, (from_a, from_b), fix_hi))):
        at, sub = (0, 0) if e == 0 else (127, 7)

        def coefficient(ref, row):
            values = ref[pl.ds((e * ROWS + row) * 8 + sub, LAYERS, stride=256), :]
            return jnp.broadcast_to(values[:, at : at + 1], (LAYERS, 128))

        deltas = []
        for row in range(ROWS):
            here = own[pl.ds(row, LAYERS, stride=ROWS), :]
            cells = pl.ds(row, LAYERS, stride=ROWS)
            there = jnp.where(even, of_even[cells, :], of_odd[cells, :])
            face = pltpu.roll(jnp.minimum(here, there), 64, 1)
            deltas.append(face * (there - here))
        rhos = [None] + [coefficient(rho, row) for row in range(1, ROWS - 1)]
        reds = [None] * ROWS
        for row in range(1, ROWS - 1):
            reds[row] = deltas[row] * coefficient(inv, row)
            if row == 1:
                total, chain = reds[1], rhos[1]
            else:
                reds[row] = reds[row] + coefficient(gain, row) * reds[row - 1]
                total = total + chain * reds[row]
                chain = chain * rhos[row]
        first = deltas[0] + coefficient(gain, 0) * total
        last = deltas[ROWS - 1] + coefficient(gain, ROWS - 1) * reds[ROWS - 2]
        zero = jnp.zeros((LAYERS, 128), F32)
        fix[pl.ds(0, LAYERS, stride=ROWS), :] = zero
        fix[pl.ds(ROWS - 1, LAYERS, stride=ROWS), :] = zero
        value = zero
        for row in reversed(range(1, ROWS - 1)):
            value = reds[row] + rhos[row] * value
            fix[pl.ds(row, LAYERS, stride=ROWS), :] = value

        def add_to(ref):
            for t in range(TRACERS):
                for part, change in ((R0 + t, first), (RN + t, last)):
                    rows = pl.ds(part * LAYERS * 8 + sub, LAYERS, stride=8)
                    ref[rows, :] = ref[rows, :] + jnp.where(lane == at, pltpu.roll(change, (at - t) % 128, 1), 0.0)

        pl.when(first_core if e == 0 else jnp.logical_not(first_core))(lambda: add_to(mine))
        pl.when(jnp.logical_not(first_core) if e == 0 else first_core)(lambda: add_to(theirs))


def outer_part(own_lo, own_hi, from_a, from_b, inv, gain, rho, mine, theirs):
    vmem = pl.BlockSpec(memory_space=pltpu.VMEM)
    flat = lambda x: x.reshape(-1, 128)
    mine, theirs, fix_lo, fix_hi = pl.pallas_call(
        outer_kernel,
        in_specs=[vmem] * 9,
        out_specs=[vmem] * 4,
        out_shape=[jax.ShapeDtypeStruct((PARTS * LAYERS * 8, 128), F32)] * 2
        + [jax.ShapeDtypeStruct((LAYERS * ROWS, 128), F32)] * 2,
        compiler_params=SMALL,
        name="outer_part",
    )(*(flat(x) for x in (own_lo, own_hi, from_a, from_b, inv, gain, rho, mine, theirs)))
    packed = (PARTS, LAYERS, 8, 128)
    return mine.reshape(packed), theirs.reshape(packed), fix_lo, fix_hi


def pair_kernel(mine, other, sent, kept):
    first_core = is_first_core()
    for l in range(LAYERS):
        a = [mine[part, l] for part in range(PARTS)]
        b = [other[part, l] for part in range(PARTS)]
        lo = [jnp.where(first_core, x, y) for x, y in zip(a, b)]
        hi = [jnp.where(first_core, y, x) for x, y in zip(a, b)]
        face = jnp.minimum(lo[CDN], hi[CD0])
        down = face + jnp.where(lo[CDN] > 0.0, hi[WA0], 0.0)
        scale = 1.0 / (lo[DN] * (hi[D0] + down) + face * hi[D0])
        in_b = scale * (hi[D0] + down)
        in_g = scale * face
        in_w = scale * down
        in_a = scale * (lo[DN] + face)
        last_f, last_l = in_b * lo[EN], in_g * hi[F0]
        first_f, first_l = in_w * lo[EN], in_a * hi[F0]
        last_r = [in_b * lo[RN + t] + in_g * hi[R0 + t] for t in range(TRACERS)]
        first_r = [in_w * lo[RN + t] + in_a * hi[R0 + t] for t in range(TRACERS)]
        out = [None] * PARTS
        out[CD0], out[WA0], out[CDN] = lo[CD0], lo[WA0], hi[CDN]
        out[D0] = lo[D0] - lo[F0] * last_f
        out[F0] = lo[F0] * last_l
        out[DN] = hi[DN] - hi[EN] * first_l
        out[EN] = hi[EN] * first_f
        for t in range(TRACERS):
            out[R0 + t] = lo[R0 + t] + lo[F0] * last_r[t]
            out[RN + t] = hi[RN + t] + hi[EN] * first_r[t]
        for part in range(PARTS):
            sent[pl.ds(l * SENT + part, CHIPS, stride=LAYERS * SENT), :] = out[part]
        sent[pl.ds(l * SENT + PARTS, CHIPS, stride=LAYERS * SENT), :] = jnp.zeros((8, 128), F32)
        for k, value in enumerate(last_r + first_r + [last_f, last_l, first_f, first_l]):
            kept[k, l] = value


def pair_part(mine, other):
    vmem = pl.BlockSpec(memory_space=pltpu.VMEM)
    return pl.pallas_call(
        pair_kernel,
        in_specs=[vmem, vmem],
        out_specs=[vmem, vmem],
        out_shape=[
            jax.ShapeDtypeStruct((CHIPS * LAYERS * SENT, 128), F32),
            jax.ShapeDtypeStruct((14, LAYERS, 8, 128), F32),
        ],
        compiler_params=SMALL,
        name="pair_part",
    )(mine, other)


def chain_kernel(parts, solved):
    load = lambda chip, part: parts[pl.ds(chip * LAYERS * SENT + part, LAYERS, stride=SENT), :]
    firsts, lasts = [], []
    cd_prev = gate = ratio = reduced = None
    base, known = None, None
    for chip in range(CHIPS):
        d0, f0 = load(chip, D0), load(chip, F0)
        dn, en = load(chip, DN), load(chip, EN)
        r0 = [load(chip, R0 + t) for t in range(TRACERS)]
        rn = [load(chip, RN + t) for t in range(TRACERS)]
        if chip:
            cd0 = load(chip, CD0)
            face = jnp.minimum(cd_prev, cd0)
            down = face + jnp.where(cd_prev > 0.0, load(chip, WA0), 0.0)
            inverse = 1.0 / (base + face)
            ratio = face * inverse
            reduced = [x * inverse for x in known]
            lasts.append((ratio, reduced))
            inverse = 1.0 / (d0 + down * (1.0 - ratio))
            r0 = [x + down * y for x, y in zip(r0, reduced)]
        else:
            inverse = 1.0 / d0
        ahead = f0 * inverse
        here = [x * inverse for x in r0]
        firsts.append((ahead, here))
        base = dn - en * ahead
        known = [x + en * y for x, y in zip(rn, here)]
        cd_prev = load(chip, CDN)
    inverse = 1.0 / base
    last = [x * inverse for x in known]
    for chip in reversed(range(CHIPS)):
        ahead, here = firsts[chip]
        first = [x + ahead * y for x, y in zip(here, last)]
        for t in range(TRACERS):
            solved[pl.ds(chip * LAYERS * BACK + t, LAYERS, stride=BACK), :] = first[t]
            solved[pl.ds(chip * LAYERS * BACK + TRACERS + t, LAYERS, stride=BACK), :] = last[t]
        if chip:
            ratio, reduced = lasts[chip - 1]
            last = [x + ratio * y for x, y in zip(reduced, first)]


def chain_part(parts):
    vmem = pl.BlockSpec(memory_space=pltpu.VMEM)
    return pl.pallas_call(
        chain_kernel,
        in_specs=[vmem],
        out_specs=vmem,
        out_shape=jax.ShapeDtypeStruct((CHIPS * LAYERS * BACK, 128), F32),
        compiler_params=SMALL,
        name="chain_part",
    )(parts)


def middle_kernel(solved, kept, mine, theirs):
    first_core = is_first_core()
    for l in range(LAYERS):
        last_f, last_l, first_f, first_l = (kept[10 + k, l] for k in range(4))
        for t in range(TRACERS):
            first = solved[pl.ds(l * BACK + t, CHIPS, stride=LAYERS * BACK), :]
            last = solved[pl.ds(l * BACK + TRACERS + t, CHIPS, stride=LAYERS * BACK), :]
            before = kept[t, l] + last_f * first + last_l * last
            after = kept[TRACERS + t, l] + first_f * first + first_l * last
            mine[t, l] = jnp.where(first_core, first, after)
            mine[TRACERS + t, l] = jnp.where(first_core, before, last)
            theirs[t, l] = jnp.where(first_core, after, first)
            theirs[TRACERS + t, l] = jnp.where(first_core, last, before)


def middle_part(solved, kept):
    vmem = pl.BlockSpec(memory_space=pltpu.VMEM)
    return pl.pallas_call(
        middle_kernel,
        in_specs=[vmem, vmem],
        out_specs=[vmem, vmem],
        out_shape=[jax.ShapeDtypeStruct((BACK, LAYERS, 8, 128), F32)] * 2,
        compiler_params=SMALL,
        name="middle_part",
    )(solved, kept)


def spread_kernel(red, fill, rho, fix_lo, fix_hi, base, of_first, of_last):
    lane = lax.broadcasted_iota(jnp.int32, (8, 128), 1)
    zero, one = jnp.zeros((8, 128), F32), jnp.ones((8, 128), F32)

    def one_layer(layer, none):
        for half in range(2):
            for row, first, last in ((0, one, zero), (ROWS - 1, zero, one)):
                of_first[layer, line(row, half), :] = first
                of_last[layer, line(row, half), :] = last
                for t in range(TRACERS):
                    base[t, layer, line(row, half), :] = zero
            values, first, last = [zero] * TRACERS, zero, one
            for row in reversed(range(1, ROWS - 1)):
                where = pl.ds((half * ROWS + row) * 8, 8)
                ratio = rho[layer, where, :]
                first = fill[layer, where, :] + ratio * first
                last = ratio * last
                of_first[layer, line(row, half), :] = first
                of_last[layer, line(row, half), :] = last
                for t in range(TRACERS):
                    values[t] = red[t, layer, where, :] + ratio * values[t]
                    base[t, layer, line(row, half), :] = values[t]
        for i in range(2):
            for fix, at, column in ((fix_lo, 0, 0), (fix_hi, 127, 15)):
                change = fix[pl.ds(layer * ROWS + i * 8, 8), :]
                for t in range(TRACERS):
                    where = tile(i, column)
                    moved = jnp.where(lane == at, pltpu.roll(change, (at - t) % 128, 1), 0.0)
                    base[t, layer, where, :] = base[t, layer, where, :] + moved

    lax.fori_loop(0, LAYERS, one_layer, None)


def spread_part(red, fill, rho, fix_lo, fix_hi):
    vmem = pl.BlockSpec(memory_space=pltpu.VMEM)
    layered = jax.ShapeDtypeStruct((LAYERS, 256, 128), F32)
    return pl.pallas_call(
        spread_kernel,
        in_specs=[vmem] * 5,
        out_specs=[vmem] * 3,
        out_shape=[jax.ShapeDtypeStruct((TRACERS, LAYERS, 256, 128), F32), layered, layered],
        compiler_params=pltpu.CompilerParams(vmem_limit_bytes=12 * 1024 * 1024),
        name="spread_part",
    )(red, fill, rho, fix_lo, fix_hi)


def final_kernel(own, base, of_first, of_last, ends, *refs):
    out, ready, sems = refs[-3:]
    half = lax.axis_index("chan") % 2
    if not own:
        half = 1 - half

    def start_of(i):
        return pl.multiple_of(i * 128 + half * 64, 64)

    def copy_of(layer, i):
        rows = pl.ds(start_of(i), 64)
        return pltpu.make_async_copy(
            ready.at[:, layer, pl.ds(i * 64, 64)], out.at[:, layer, rows], sems.at[layer, i]
        )

    def one_layer(layer, none):
        for j in range(8):
            spread = lambda k: jnp.broadcast_to(ends[k, layer, pl.ds(j, 1), :], (8, 128))
            firsts = [spread(t) for t in range(TRACERS)]
            lasts = [spread(TRACERS + t) for t in range(TRACERS)]
            for i in range(2):
                where = pl.ds(pl.multiple_of(start_of(i) + j * 8, 8), 8)
                by_first, by_last = of_first[layer, where, :], of_last[layer, where, :]
                for t in range(TRACERS):
                    ready[t, layer, pl.ds(i * 64 + j * 8, 8), :] = (
                        base[t, layer, where, :] + by_first * firsts[t] + by_last * lasts[t]
                    )
        for i in range(2):
            copy_of(layer, i).start()

    lax.fori_loop(0, LAYERS, one_layer, None)
    for layer in range(LAYERS):
        for i in range(2):
            copy_of(layer, i).wait()


def final_part(base, of_first, of_last, ends, partial=None):
    vmem = pl.BlockSpec(memory_space=pltpu.VMEM)
    hbm = pl.BlockSpec(memory_space=pltpu.HBM)
    own = partial is None
    return pl.pallas_call(
        functools.partial(final_kernel, own),
        in_specs=[vmem] * 4 + ([] if own else [hbm]),
        out_specs=hbm,
        out_shape=jax.ShapeDtypeStruct((TRACERS, LAYERS, 256, 128), F32),
        input_output_aliases={} if own else {4: 0},
        scratch_shapes=[
            pltpu.VMEM((TRACERS, LAYERS, 128, 128), F32),
            pltpu.SemaphoreType.DMA((LAYERS, 2)),
        ],
        compiler_params=pltpu.CompilerParams(vmem_limit_bytes=8 * 1024 * 1024),
        name="final_own" if own else "final_other",
    )(base, of_first, of_last, ends, *(() if own else (partial,)))


def on_device(tracers, kappa_x, kappa_y, courant, wet_mask, levels):
    count = lax.axis_size("cross")
    pairs = [(i, i ^ 1) for i in range(2 * CHIPS)]
    lines = [[c + 2 * z for z in range(CHIPS)] for c in range(2)]

    lowest, highest, to_a, to_b = edges(tracers, kappa_y, wet_mask, levels)
    swap_a = [(i, i ^ 1) for i in range(count)]
    swap_b = []
    for along in range(2 * CHIPS):
        for i in range(count):
            inner = 0 < i < count - 1
            partner = along * count + ((i + 1) ^ 1) - 1 if inner else (along ^ 1) * count + i
            swap_b.append((along * count + i, partner))
    from_b = inner_part(lax.ppermute(to_b, ("chan", "cross"), swap_b))
    from_a = lax.ppermute(to_a, "cross", swap_a)
    red, fill, rho, inv, gain, mine, theirs = local_part(
        folded(tracers),
        folded(kappa_x),
        folded(kappa_y),
        folded(courant),
        folded(wet_mask),
        folded(levels),
    )
    mine, theirs, fix_lo, fix_hi = outer_part(
        lowest, highest, from_a, from_b, inv, gain, rho, mine, theirs
    )
    other = lax.ppermute(theirs, "chan", pairs)
    base, of_first, of_last = spread_part(red, fill, rho, fix_lo, fix_hi)
    other, base, of_first, of_last = lax.optimization_barrier((other, base, of_first, of_last))
    sent, kept = pair_part(mine, other)
    parts = lax.all_to_all(
        sent.reshape(CHIPS, LAYERS * SENT, 128), "chan", 0, 0, axis_index_groups=lines, tiled=True
    )
    solved = chain_part(parts.reshape(CHIPS * LAYERS * SENT, 128))
    back = lax.all_to_all(
        solved.reshape(CHIPS, LAYERS * BACK, 128), "chan", 0, 0, axis_index_groups=lines, tiled=True
    )
    mine, theirs = middle_part(back.reshape(CHIPS * LAYERS * BACK, 128), kept)
    other = lax.ppermute(theirs, "chan", pairs)
    partial = final_part(base, of_first, of_last, mine)
    return unfolded(final_part(base, of_first, of_last, other, partial))


def solution(mesh):
    placed = (
        P(None, None, "chan", "cross"),
        P(None, "chan", "cross"),
        P(None, "chan", "cross"),
        P(None, "chan", "cross"),
        P("chan", "cross"),
        P("chan", "cross"),
    )
    return jax.shard_map(
        on_device,
        mesh=mesh,
        in_specs=placed,
        out_specs=P(None, None, "chan", "cross"),
        check_vma=False,
    )
```

```python
import functools

import jax
import jax.numpy as jnp
from jax import lax
from jax.experimental import pallas as pl
from jax.experimental.pallas import tpu as pltpu
from jax.sharding import PartitionSpec as P

TRACERS = 5
LAYERS = 4
ROWS = 16
CHIPS = 8
CD0, WA0, D0, F0, R0, CDN, DN, EN, RN = 0, 1, 2, 3, 4, 9, 10, 11, 12
PARTS = 17
SENT = 18
BACK = 10
F32 = jnp.float32
SMALL = pltpu.CompilerParams(vmem_limit_bytes=4 * 1024 * 1024)


def folded(cells):
    lead = cells.shape[:-2]
    cells = cells.reshape(lead + (2, 8, 16, 128))
    return jnp.swapaxes(cells, len(lead) + 1, len(lead) + 2).reshape(lead + (256, 128))


def unfolded(cells):
    lead = cells.shape[:-2]
    cells = cells.reshape(lead + (2, 16, 8, 128))
    return jnp.swapaxes(cells, len(lead) + 1, len(lead) + 2).reshape(lead + (16, 2048))


def in_hbm(cells):
    return pltpu.with_memory_space_constraint(cells, pltpu.HBM)


def line(row, half):
    return pl.ds((row // 8) * 128 + half * 64 + row % 8, 8, stride=8)


def is_first_core():
    return lax.axis_index("chan") % 2 == 0


def tile(row_tile, column_tile):
    return pl.ds(row_tile * 128 + column_tile * 8, 8)


def edges_kernel(
    tr_lo, tr_hi, ky_lo, ky_hi, wet_lo, wet_hi, lev_lo, lev_hi, out_lo, out_hi, swap_a, swap_b
):
    even = lax.axis_index("cross") % 2 == 0
    lane = lax.broadcasted_iota(jnp.int32, (8, 128), 1)
    for i in range(2):
        rows = pl.ds(i * 8, 8)
        sent = []
        for tr, ky, wet, lev, out, at in (
            (tr_lo, ky_lo, wet_lo, lev_lo, out_lo, 0),
            (tr_hi, ky_hi, wet_hi, lev_hi, out_hi, 127),
        ):
            together = jnp.zeros((8, 128), F32)
            for l in range(LAYERS):
                active = (wet[rows, :] > 0) & (lev[rows, :] > l)
                cross = jnp.where(active, ky[l, rows, :], 0.0)
                packed = jnp.where(lane < 8, 0.0, jnp.broadcast_to(cross[:, at : at + 1], (8, 128)))
                for t in range(TRACERS):
                    packed = jnp.where(lane == t, pltpu.roll(tr[t, l, rows, :], (t - at) % 128, 1), packed)
                out[l, rows, :] = packed
                moved = packed if l == 0 else pltpu.roll(packed, 16 * l, 1)
                together = jnp.where(lane // 16 == l, moved, together)
            sent.append(together)
        lo, hi = sent
        swap_a[rows, :] = jnp.where(even, hi, lo)
        swap_b[rows, :] = jnp.where(even, lo, hi)


def edges(tracers, kappa_y, wet, levels):
    def spec(lead, at):
        zeros = (0,) * (len(lead) + 1)
        return pl.BlockSpec(lead + (16, 128), lambda i, zeros=zeros, at=at: zeros + (at,))

    return pl.pallas_call(
        edges_kernel,
        grid=(1,),
        in_specs=[
            spec((TRACERS, LAYERS), 0),
            spec((TRACERS, LAYERS), 15),
            spec((LAYERS,), 0),
            spec((LAYERS,), 15),
            spec((), 0),
            spec((), 15),
            spec((), 0),
            spec((), 15),
        ],
        out_specs=[pl.BlockSpec((LAYERS, 16, 128), lambda i: (0, 0, 0))] * 2
        + [pl.BlockSpec((16, 128), lambda i: (0, 0))] * 2,
        out_shape=[jax.ShapeDtypeStruct((LAYERS, 16, 128), F32)] * 2
        + [jax.ShapeDtypeStruct((16, 128), F32)] * 2,
        compiler_params=SMALL,
        name="edges",
    )(*(in_hbm(x) for x in (tracers, tracers, kappa_y, kappa_y, wet, wet, levels, levels)))


def local_kernel(
    tr, kx_hbm, ky, co_hbm, wet, lev, red, fill, rho, inv, gain, mine, theirs, side, kx, co, shift, moved, sems
):
    copies = [
        pltpu.make_async_copy(kx_hbm, kx, sems.at[0]),
        pltpu.make_async_copy(co_hbm, co, sems.at[1]),
    ]
    for copy in copies:
        copy.start()
    source = lax.broadcasted_iota(jnp.int32, (256, 256), 0) % 128
    target = lax.broadcasted_iota(jnp.int32, (256, 256), 1)
    wanted = jnp.where(target < 128, target + 1, target + 127) % 128
    shift[...] = jnp.where(source == wanted, 1.0, 0.0).astype(jnp.bfloat16)
    for layer in range(LAYERS):
        right_sides(layer, tr, ky, wet, lev, side, shift, moved.at[layer % 2])
    for copy in copies:
        copy.wait()
    eliminate_bands(kx, co, wet, lev, fill, rho, inv, gain, mine, theirs)
    lax.fori_loop(
        0, LAYERS, lambda layer, none: eliminate_sides(layer, red, rho, inv, gain, mine, theirs, side), None
    )


def right_sides(layer, tr, ky, wet, lev, side, shift, moved):
    lane = lax.broadcasted_iota(jnp.int32, (8, 128), 1)
    head, tail = lane == 0, lane == 127

    def move(k, cells):
        coarse = cells.astype(jnp.bfloat16)
        rest = (cells - coarse.astype(F32)).astype(jnp.bfloat16)
        moved[k] = jnp.dot(
            jnp.concatenate([coarse, rest], axis=1), shift[...], preferred_element_type=F32
        )

    def ahead(k, i, j):
        here = moved[k, tile(i, j), 0:128]
        return here if j == 15 else jnp.where(tail, moved[k, tile(i, j + 1), 0:128], here)

    def behind(k, i, j):
        here = moved[k, tile(i, j), 128:256]
        return here if j == 0 else jnp.where(head, moved[k, tile(i, j - 1), 128:256], here)

    cross = jnp.where((wet[...] > 0) & (lev[...] > layer), ky[layer], 0.0)
    move(TRACERS, cross)
    for t in range(TRACERS):
        move(t, tr[t, layer])
    for i in range(2):
        for j in range(16):
            now = cross[i * 128 + j * 8 : i * 128 + j * 8 + 8]
            upper = jnp.minimum(now, ahead(TRACERS, i, j))
            lower = jnp.minimum(now, behind(TRACERS, i, j))
            if j == 15:
                upper = jnp.where(tail, 0.0, upper)
            if j == 0:
                lower = jnp.where(head, 0.0, lower)
            for t in range(TRACERS):
                centre = tr[t, layer, tile(i, j), :]
                side[layer, t, tile(i, j), :] = (
                    centre + upper * (ahead(t, i, j) - centre) - lower * (centre - behind(t, i, j))
                )


def row_of(half, row):
    return pl.ds((half * ROWS + row) * 8, 8)


def put(mine, theirs, part, layer, halves):
    first_core = is_first_core()
    mine[part, layer] = jnp.where(first_core, halves[0], halves[1])
    theirs[part, layer] = jnp.where(first_core, halves[1], halves[0])


def eliminate_bands(kx, co, wet, lev, fill, rho, inv, gain, mine, theirs):
    groups = [(layer, half) for layer in range(LAYERS) for half in range(2)]
    depth = [lev[line(0, half), :] for half in range(2)]
    deep = {g: depth[g[1]] > g[0] for g in groups}

    def load(row):
        diff, flow = {}, {}
        for half in range(2):
            where = line(row, half)
            water = wet[where, :] > 0
            for layer in range(LAYERS):
                g = layer, half
                active = water & deep[g]
                diff[g] = jnp.where(active, kx[layer, where, :], 0.0)
                flow[g] = jnp.where(active, co[layer, where, :], 0.0)
        return diff, flow

    def put_all(part, values):
        for layer in range(LAYERS):
            put(mine, theirs, part, layer, [values[layer, half] for half in range(2)])

    before, flow = load(0)
    put_all(CD0, before)
    put_all(WA0, flow)
    now, flow = load(1)
    first = {g: jnp.minimum(before[g], now[g]) for g in groups}
    for layer, half in groups:
        gain[layer, row_of(half, 0), :] = first[layer, half]
    down = dict(first)
    ratio, fills, sums, chain = {}, {}, {}, {}
    for row in range(1, ROWS - 1):
        after, flow_after = load(row + 1)
        for g in groups:
            layer, half = g
            where = row_of(half, row)
            up = jnp.minimum(now[g], after[g])
            low = down[g] + jnp.where(before[g] > 0.0, flow[g], 0.0)
            if row == 1:
                inverse = 1.0 / (1.0 + up + low)
                ratio[g] = up * inverse
                gained = low * inverse
                fills[g] = gained
                sums[g] = gained
                chain[g] = ratio[g]
            else:
                inverse = 1.0 / (1.0 + up + low * (1.0 - ratio[g]))
                ratio[g] = up * inverse
                gained = low * inverse
                fills[g] = gained * fills[g]
                sums[g] = sums[g] + chain[g] * fills[g]
                chain[g] = chain[g] * ratio[g]
            inv[layer, where, :] = inverse
            gain[layer, where, :] = gained
            rho[layer, where, :] = ratio[g]
            fill[layer, where, :] = fills[g]
            down[g] = up
        before, now, flow = now, after, flow_after
    low = {g: down[g] + jnp.where(before[g] > 0.0, flow[g], 0.0) for g in groups}
    for layer, half in groups:
        gain[layer, row_of(half, ROWS - 1), :] = low[layer, half]
    put_all(CDN, now)
    put_all(D0, {g: 1.0 + first[g] * (1.0 - sums[g]) for g in groups})
    put_all(F0, {g: first[g] * chain[g] for g in groups})
    put_all(DN, {g: 1.0 + low[g] * (1.0 - ratio[g]) for g in groups})
    put_all(EN, {g: low[g] * fills[g] for g in groups})


def eliminate_sides(layer, red, rho, inv, gain, mine, theirs, side):
    edges_of = []
    for half in range(2):
        get = lambda t, row: side[layer, t, line(row, half), :]
        for row in range(1, ROWS - 1):
            where = row_of(half, row)
            inverse, ratio = inv[layer, where, :], rho[layer, where, :]
            if row == 1:
                reds = [get(t, row) * inverse for t in range(TRACERS)]
                sums = list(reds)
                chain = ratio
            else:
                gained = gain[layer, where, :]
                reds = [get(t, row) * inverse + gained * reds[t] for t in range(TRACERS)]
                sums = [sums[t] + chain * reds[t] for t in range(TRACERS)]
                chain = chain * ratio
            for t in range(TRACERS):
                red[t, layer, where, :] = reds[t]
        first, low = gain[layer, row_of(half, 0), :], gain[layer, row_of(half, ROWS - 1), :]
        edges_of.append(
            [get(t, 0) + first * sums[t] for t in range(TRACERS)]
            + [get(t, ROWS - 1) + low * reds[t] for t in range(TRACERS)]
        )
    for t in range(TRACERS):
        for part, k in ((R0 + t, t), (RN + t, TRACERS + t)):
            put(mine, theirs, part, layer, [edges_of[0][k], edges_of[1][k]])


def local_part(tracers, kappa_x, kappa_y, courant, wet, levels):
    vmem = pl.BlockSpec(memory_space=pltpu.VMEM)
    hbm = pl.BlockSpec(memory_space=pltpu.HBM)
    layered = jax.ShapeDtypeStruct((LAYERS, 256, 128), F32)
    packed = jax.ShapeDtypeStruct((PARTS, LAYERS, 8, 128), F32)
    return pl.pallas_call(
        local_kernel,
        in_specs=[vmem, hbm, vmem, hbm, vmem, vmem],
        out_specs=[vmem] * 7,
        out_shape=[jax.ShapeDtypeStruct((TRACERS, LAYERS, 256, 128), F32)] + [layered] * 4 + [packed] * 2,
        scratch_shapes=[
            pltpu.VMEM((LAYERS, TRACERS, 256, 128), F32),
            pltpu.VMEM((LAYERS, 256, 128), F32),
            pltpu.VMEM((LAYERS, 256, 128), F32),
            pltpu.VMEM((256, 256), jnp.bfloat16),
            pltpu.VMEM((2, TRACERS + 1, 256, 256), F32),
            pltpu.SemaphoreType.DMA((2,)),
        ],
        compiler_params=pltpu.CompilerParams(vmem_limit_bytes=12 * 1024 * 1024),
        name="local_part",
    )(tracers, in_hbm(kappa_x), kappa_y, in_hbm(courant), wet, levels)


def unpacked(cells, l):
    return cells if l == 0 else pltpu.roll(cells, 128 - 16 * l, 1)


def inner_kernel(cells, out):
    place = lax.axis_index("cross")
    inner = (place > 0) & (place < lax.axis_size("cross") - 1)
    for l in range(LAYERS):
        out[l * ROWS : (l + 1) * ROWS, :] = jnp.where(inner, unpacked(cells[...], l), 0.0)


def inner_part(cells):
    vmem = pl.BlockSpec(memory_space=pltpu.VMEM)
    return pl.pallas_call(
        inner_kernel,
        in_specs=[vmem],
        out_specs=vmem,
        out_shape=jax.ShapeDtypeStruct((LAYERS * ROWS, 128), F32),
        compiler_params=SMALL,
        name="inner_part",
    )(cells)


def outer_kernel(
    own_lo, own_hi, sent_a, from_b, inv, gain, rho, mine_in, theirs_in, mine, theirs, fix_lo, fix_hi, from_a
):
    even = lax.axis_index("cross") % 2 == 0
    first_core = is_first_core()
    for l in range(LAYERS):
        from_a[l * ROWS : (l + 1) * ROWS, :] = unpacked(sent_a[...], l)
    mine[...] = mine_in[...]
    theirs[...] = theirs_in[...]
    lane = lax.broadcasted_iota(jnp.int32, (LAYERS, 128), 1)
    for e, (own, (of_even, of_odd), fix) in enumerate(((own_lo, (from_b, from_a), fix_lo), (own_hi, (from_a, from_b), fix_hi))):
        at, sub = (0, 0) if e == 0 else (127, 7)

        def coefficient(ref, row):
            values = ref[pl.ds((e * ROWS + row) * 8 + sub, LAYERS, stride=256), :]
            return jnp.broadcast_to(values[:, at : at + 1], (LAYERS, 128))

        deltas = []
        for row in range(ROWS):
            here = own[pl.ds(row, LAYERS, stride=ROWS), :]
            cells = pl.ds(row, LAYERS, stride=ROWS)
            there = jnp.where(even, of_even[cells, :], of_odd[cells, :])
            face = pltpu.roll(jnp.minimum(here, there), 120, 1)
            deltas.append(face * (there - here))
        rhos = [None] + [coefficient(rho, row) for row in range(1, ROWS - 1)]
        reds = [None] * ROWS
        for row in range(1, ROWS - 1):
            reds[row] = deltas[row] * coefficient(inv, row)
            if row == 1:
                total, chain = reds[1], rhos[1]
            else:
                reds[row] = reds[row] + coefficient(gain, row) * reds[row - 1]
                total = total + chain * reds[row]
                chain = chain * rhos[row]
        first = deltas[0] + coefficient(gain, 0) * total
        last = deltas[ROWS - 1] + coefficient(gain, ROWS - 1) * reds[ROWS - 2]
        zero = jnp.zeros((LAYERS, 128), F32)
        fix[pl.ds(0, LAYERS, stride=ROWS), :] = zero
        fix[pl.ds(ROWS - 1, LAYERS, stride=ROWS), :] = zero
        value = zero
        for row in reversed(range(1, ROWS - 1)):
            value = reds[row] + rhos[row] * value
            fix[pl.ds(row, LAYERS, stride=ROWS), :] = value

        def add_to(ref):
            for t in range(TRACERS):
                for part, change in ((R0 + t, first), (RN + t, last)):
                    rows = pl.ds(part * LAYERS * 8 + sub, LAYERS, stride=8)
                    ref[rows, :] = ref[rows, :] + jnp.where(lane == at, pltpu.roll(change, (at - t) % 128, 1), 0.0)

        pl.when(first_core if e == 0 else jnp.logical_not(first_core))(lambda: add_to(mine))
        pl.when(jnp.logical_not(first_core) if e == 0 else first_core)(lambda: add_to(theirs))


def outer_part(own_lo, own_hi, from_a, from_b, inv, gain, rho, mine, theirs):
    vmem = pl.BlockSpec(memory_space=pltpu.VMEM)
    flat = lambda x: x.reshape(-1, 128)
    mine, theirs, fix_lo, fix_hi = pl.pallas_call(
        outer_kernel,
        in_specs=[vmem] * 9,
        out_specs=[vmem] * 4,
        out_shape=[jax.ShapeDtypeStruct((PARTS * LAYERS * 8, 128), F32)] * 2
        + [jax.ShapeDtypeStruct((LAYERS * ROWS, 128), F32)] * 2,
        scratch_shapes=[pltpu.VMEM((LAYERS * ROWS, 128), F32)],
        compiler_params=SMALL,
        name="outer_part",
    )(*(flat(x) for x in (own_lo, own_hi, from_a, from_b, inv, gain, rho, mine, theirs)))
    packed = (PARTS, LAYERS, 8, 128)
    return mine.reshape(packed), theirs.reshape(packed), fix_lo, fix_hi


def pair_kernel(mine, other, sent, kept):
    first_core = is_first_core()
    for l in range(LAYERS):
        a = [mine[part, l] for part in range(PARTS)]
        b = [other[part, l] for part in range(PARTS)]
        lo = [jnp.where(first_core, x, y) for x, y in zip(a, b)]
        hi = [jnp.where(first_core, y, x) for x, y in zip(a, b)]
        face = jnp.minimum(lo[CDN], hi[CD0])
        down = face + jnp.where(lo[CDN] > 0.0, hi[WA0], 0.0)
        scale = 1.0 / (lo[DN] * (hi[D0] + down) + face * hi[D0])
        in_b = scale * (hi[D0] + down)
        in_g = scale * face
        in_w = scale * down
        in_a = scale * (lo[DN] + face)
        last_f, last_l = in_b * lo[EN], in_g * hi[F0]
        first_f, first_l = in_w * lo[EN], in_a * hi[F0]
        last_r = [in_b * lo[RN + t] + in_g * hi[R0 + t] for t in range(TRACERS)]
        first_r = [in_w * lo[RN + t] + in_a * hi[R0 + t] for t in range(TRACERS)]
        out = [None] * PARTS
        out[CD0], out[WA0], out[CDN] = lo[CD0], lo[WA0], hi[CDN]
        out[D0] = lo[D0] - lo[F0] * last_f
        out[F0] = lo[F0] * last_l
        out[DN] = hi[DN] - hi[EN] * first_l
        out[EN] = hi[EN] * first_f
        for t in range(TRACERS):
            out[R0 + t] = lo[R0 + t] + lo[F0] * last_r[t]
            out[RN + t] = hi[RN + t] + hi[EN] * first_r[t]
        for part in range(PARTS):
            sent[pl.ds(l * SENT + part, CHIPS, stride=LAYERS * SENT), :] = out[part]
        sent[pl.ds(l * SENT + PARTS, CHIPS, stride=LAYERS * SENT), :] = jnp.zeros((8, 128), F32)
        for k, value in enumerate(last_r + first_r + [last_f, last_l, first_f, first_l]):
            kept[k, l] = value


def pair_part(mine, other):
    vmem = pl.BlockSpec(memory_space=pltpu.VMEM)
    return pl.pallas_call(
        pair_kernel,
        in_specs=[vmem, vmem],
        out_specs=[vmem, vmem],
        out_shape=[
            jax.ShapeDtypeStruct((CHIPS * LAYERS * SENT, 128), F32),
            jax.ShapeDtypeStruct((14, LAYERS, 8, 128), F32),
        ],
        compiler_params=SMALL,
        name="pair_part",
    )(mine, other)


def chain_kernel(parts, solved):
    load = lambda chip, part: parts[pl.ds(chip * LAYERS * SENT + part, LAYERS, stride=SENT), :]
    firsts, lasts = [], []
    cd_prev = gate = ratio = reduced = None
    base, known = None, None
    for chip in range(CHIPS):
        d0, f0 = load(chip, D0), load(chip, F0)
        dn, en = load(chip, DN), load(chip, EN)
        r0 = [load(chip, R0 + t) for t in range(TRACERS)]
        rn = [load(chip, RN + t) for t in range(TRACERS)]
        if chip:
            cd0 = load(chip, CD0)
            face = jnp.minimum(cd_prev, cd0)
            down = face + jnp.where(cd_prev > 0.0, load(chip, WA0), 0.0)
            inverse = 1.0 / (base + face)
            ratio = face * inverse
            reduced = [x * inverse for x in known]
            lasts.append((ratio, reduced))
            inverse = 1.0 / (d0 + down * (1.0 - ratio))
            r0 = [x + down * y for x, y in zip(r0, reduced)]
        else:
            inverse = 1.0 / d0
        ahead = f0 * inverse
        here = [x * inverse for x in r0]
        firsts.append((ahead, here))
        base = dn - en * ahead
        known = [x + en * y for x, y in zip(rn, here)]
        cd_prev = load(chip, CDN)
    inverse = 1.0 / base
    last = [x * inverse for x in known]
    for chip in reversed(range(CHIPS)):
        ahead, here = firsts[chip]
        first = [x + ahead * y for x, y in zip(here, last)]
        for t in range(TRACERS):
            solved[pl.ds(chip * LAYERS * BACK + t, LAYERS, stride=BACK), :] = first[t]
            solved[pl.ds(chip * LAYERS * BACK + TRACERS + t, LAYERS, stride=BACK), :] = last[t]
        if chip:
            ratio, reduced = lasts[chip - 1]
            last = [x + ratio * y for x, y in zip(reduced, first)]


def chain_part(parts):
    vmem = pl.BlockSpec(memory_space=pltpu.VMEM)
    return pl.pallas_call(
        chain_kernel,
        in_specs=[vmem],
        out_specs=vmem,
        out_shape=jax.ShapeDtypeStruct((CHIPS * LAYERS * BACK, 128), F32),
        compiler_params=SMALL,
        name="chain_part",
    )(parts)


def middle_kernel(solved, kept, mine, theirs):
    first_core = is_first_core()
    for l in range(LAYERS):
        last_f, last_l, first_f, first_l = (kept[10 + k, l] for k in range(4))
        for t in range(TRACERS):
            first = solved[pl.ds(l * BACK + t, CHIPS, stride=LAYERS * BACK), :]
            last = solved[pl.ds(l * BACK + TRACERS + t, CHIPS, stride=LAYERS * BACK), :]
            before = kept[t, l] + last_f * first + last_l * last
            after = kept[TRACERS + t, l] + first_f * first + first_l * last
            mine[t, l] = jnp.where(first_core, first, after)
            mine[TRACERS + t, l] = jnp.where(first_core, before, last)
            theirs[t, l] = jnp.where(first_core, after, first)
            theirs[TRACERS + t, l] = jnp.where(first_core, last, before)


def middle_part(solved, kept):
    vmem = pl.BlockSpec(memory_space=pltpu.VMEM)
    return pl.pallas_call(
        middle_kernel,
        in_specs=[vmem, vmem],
        out_specs=[vmem, vmem],
        out_shape=[jax.ShapeDtypeStruct((BACK, LAYERS, 8, 128), F32)] * 2,
        compiler_params=SMALL,
        name="middle_part",
    )(solved, kept)


def spread_kernel(red, fill, rho, fix_lo, fix_hi, base, of_first, of_last):
    lane = lax.broadcasted_iota(jnp.int32, (8, 128), 1)
    zero, one = jnp.zeros((8, 128), F32), jnp.ones((8, 128), F32)

    def one_layer(layer, none):
        for half in range(2):
            for row, first, last in ((0, one, zero), (ROWS - 1, zero, one)):
                of_first[layer, line(row, half), :] = first
                of_last[layer, line(row, half), :] = last
                for t in range(TRACERS):
                    base[t, layer, line(row, half), :] = zero
            values, first, last = [zero] * TRACERS, zero, one
            for row in reversed(range(1, ROWS - 1)):
                where = pl.ds((half * ROWS + row) * 8, 8)
                ratio = rho[layer, where, :]
                first = fill[layer, where, :] + ratio * first
                last = ratio * last
                of_first[layer, line(row, half), :] = first
                of_last[layer, line(row, half), :] = last
                for t in range(TRACERS):
                    values[t] = red[t, layer, where, :] + ratio * values[t]
                    base[t, layer, line(row, half), :] = values[t]
        for i in range(2):
            for fix, at, column in ((fix_lo, 0, 0), (fix_hi, 127, 15)):
                change = fix[pl.ds(layer * ROWS + i * 8, 8), :]
                for t in range(TRACERS):
                    where = tile(i, column)
                    moved = jnp.where(lane == at, pltpu.roll(change, (at - t) % 128, 1), 0.0)
                    base[t, layer, where, :] = base[t, layer, where, :] + moved

    lax.fori_loop(0, LAYERS, one_layer, None)


def spread_part(red, fill, rho, fix_lo, fix_hi):
    vmem = pl.BlockSpec(memory_space=pltpu.VMEM)
    layered = jax.ShapeDtypeStruct((LAYERS, 256, 128), F32)
    return pl.pallas_call(
        spread_kernel,
        in_specs=[vmem] * 5,
        out_specs=[vmem] * 3,
        out_shape=[jax.ShapeDtypeStruct((TRACERS, LAYERS, 256, 128), F32), layered, layered],
        compiler_params=pltpu.CompilerParams(vmem_limit_bytes=12 * 1024 * 1024),
        name="spread_part",
    )(red, fill, rho, fix_lo, fix_hi)


def final_kernel(own, base, of_first, of_last, ends, *refs):
    out, ready, sems = refs[-3:]
    half = lax.axis_index("chan") % 2
    if not own:
        half = 1 - half

    def start_of(i):
        return pl.multiple_of(i * 128 + half * 64, 64)

    def copy_of(layer, i):
        rows = pl.ds(start_of(i), 64)
        return pltpu.make_async_copy(
            ready.at[:, layer, pl.ds(i * 64, 64)], out.at[:, layer, rows], sems.at[layer, i]
        )

    def one_layer(layer, none):
        for j in range(8):
            spread = lambda k: jnp.broadcast_to(ends[k, layer, pl.ds(j, 1), :], (8, 128))
            firsts = [spread(t) for t in range(TRACERS)]
            lasts = [spread(TRACERS + t) for t in range(TRACERS)]
            for i in range(2):
                where = pl.ds(pl.multiple_of(start_of(i) + j * 8, 8), 8)
                by_first, by_last = of_first[layer, where, :], of_last[layer, where, :]
                for t in range(TRACERS):
                    ready[t, layer, pl.ds(i * 64 + j * 8, 8), :] = (
                        base[t, layer, where, :] + by_first * firsts[t] + by_last * lasts[t]
                    )
        for i in range(2):
            copy_of(layer, i).start()

    lax.fori_loop(0, LAYERS, one_layer, None)
    for layer in range(LAYERS):
        for i in range(2):
            copy_of(layer, i).wait()


def final_part(base, of_first, of_last, ends, partial=None):
    vmem = pl.BlockSpec(memory_space=pltpu.VMEM)
    hbm = pl.BlockSpec(memory_space=pltpu.HBM)
    own = partial is None
    return pl.pallas_call(
        functools.partial(final_kernel, own),
        in_specs=[vmem] * 4 + ([] if own else [hbm]),
        out_specs=hbm,
        out_shape=jax.ShapeDtypeStruct((TRACERS, LAYERS, 256, 128), F32),
        input_output_aliases={} if own else {4: 0},
        scratch_shapes=[
            pltpu.VMEM((TRACERS, LAYERS, 128, 128), F32),
            pltpu.SemaphoreType.DMA((LAYERS, 2)),
        ],
        compiler_params=pltpu.CompilerParams(vmem_limit_bytes=8 * 1024 * 1024),
        name="final_own" if own else "final_other",
    )(base, of_first, of_last, ends, *(() if own else (partial,)))


def on_device(tracers, kappa_x, kappa_y, courant, wet_mask, levels):
    count = lax.axis_size("cross")
    pairs = [(i, i ^ 1) for i in range(2 * CHIPS)]
    lines = [[c + 2 * z for z in range(CHIPS)] for c in range(2)]

    lowest, highest, to_a, to_b = edges(tracers, kappa_y, wet_mask, levels)
    swap_a = [(i, i ^ 1) for i in range(count)]
    swap_b = []
    for along in range(2 * CHIPS):
        for i in range(count):
            inner = 0 < i < count - 1
            partner = along * count + ((i + 1) ^ 1) - 1 if inner else (along ^ 1) * count + i
            swap_b.append((along * count + i, partner))
    from_b = inner_part(lax.ppermute(to_b, ("chan", "cross"), swap_b))
    from_a = lax.ppermute(to_a, "cross", swap_a)
    red, fill, rho, inv, gain, mine, theirs = local_part(
        folded(tracers),
        folded(kappa_x),
        folded(kappa_y),
        folded(courant),
        folded(wet_mask),
        folded(levels),
    )
    mine, theirs, fix_lo, fix_hi = outer_part(
        lowest, highest, from_a, from_b, inv, gain, rho, mine, theirs
    )
    other = lax.ppermute(theirs, "chan", pairs)
    base, of_first, of_last = spread_part(red, fill, rho, fix_lo, fix_hi)
    other, base, of_first, of_last = lax.optimization_barrier((other, base, of_first, of_last))
    sent, kept = pair_part(mine, other)
    parts = lax.all_to_all(
        sent.reshape(CHIPS, LAYERS * SENT, 128), "chan", 0, 0, axis_index_groups=lines, tiled=True
    )
    solved = chain_part(parts.reshape(CHIPS * LAYERS * SENT, 128))
    back = lax.all_to_all(
        solved.reshape(CHIPS, LAYERS * BACK, 128), "chan", 0, 0, axis_index_groups=lines, tiled=True
    )
    mine, theirs = middle_part(back.reshape(CHIPS * LAYERS * BACK, 128), kept)
    other = lax.ppermute(theirs, "chan", pairs)
    partial = final_part(base, of_first, of_last, mine)
    return unfolded(final_part(base, of_first, of_last, other, partial))


def solution(mesh):
    placed = (
        P(None, None, "chan", "cross"),
        P(None, "chan", "cross"),
        P(None, "chan", "cross"),
        P(None, "chan", "cross"),
        P("chan", "cross"),
        P("chan", "cross"),
    )
    return jax.shard_map(
        on_device,
        mesh=mesh,
        in_specs=placed,
        out_specs=P(None, None, "chan", "cross"),
        check_vma=False,
    )
```
